128 devices in a mesh: dp: 4 (over z), expert: 8 (over y, core), tensor: 4 (over x).
Axes of the slice: x: 4, y: 4, z: 4, core: 2. Of those that a mesh axis runs over, the one named last changes fastest.
Arguments:
- attn: bfloat16 [16384, 8192], P(('dp', 'expert'), 'tensor'), parts along dimension 0, may hold values from -6 to 6
- w_out: bfloat16 [8192, 5120], P('tensor', 'expert'), may hold values from -0.0625 to 0.0625
- resid: bfloat16 [16384, 5120], P(('dp', 'expert', 'tensor')), parts along dimension 0, may hold values from -40 to 40
- norm_gain: float32 [5120], replicated, may hold values from 0.1 to 1.9
- route_ids: int32 [16384, 1], P(('dp', 'expert', 'tensor')), parts along dimension 0, may hold values from 0 to 7, as said below
- gate_vals: float32 [16384, 1], P(('dp', 'expert', 'tensor')), parts along dimension 0, may hold values from 0.2 to 1
- w_gate: bfloat16 [8, 5120, 1536], P('expert', None, 'tensor'), may hold values from -0.078125 to 0.078125
- w_up: bfloat16 [8, 5120, 1536], P('expert', None, 'tensor'), may hold values from -0.078125 to 0.078125
- w_down: bfloat16 [8, 1536, 5120], P('expert', 'tensor'), may hold values from -0.15625 to 0.15625
Outputs:
- layer_out: bfloat16 [16384, 5120], P(('dp', 'expert', 'tensor')), parts along dimension 0
The draws below stay inside these ranges and needn't reach their ends.
There are 4 independent parts, one for each index of `dp`. The reference program is written for one: setup_inputs(seed, part) draws one part's arguments, and reference() takes and returns one part's arrays. A program takes and returns all parts, laid end to end along the dimension named above; an argument that names none is the same for every part. Nothing has to cross between parts.
Inputs may be any that keep to these rules, and one draw needn't show every extreme that they name: `route_ids`: A row names 1 different experts. In each aligned block of 128 rows (the rows of one device) no expert is named by more than 24 rows, and one expert is named by exactly 24 rows in every block.
All inputs are finite; a program needn't handle non-finite values.
Results may differ from the reference program's by a relative error of at most 0.01.
Values may be sent and summed in bfloat16 or wider, within the bound.
A program may use at most 128 MiB of HBM per device.

```python
import math
import jax
import jax.numpy as jnp
from jax import lax

D = 5120
FF = 1536
HDIM = 128
HEADS = 64
TOPK = 1
ROWS = 128
EXPERTS = 8
CAP = 24
TOKENS = 4096
N_EXPERT = 8
N_TENSOR = 4


def draw_resid(key, part):
    key = jax.random.fold_in(key, 5)
    key_base, key_rows, key_cols = jax.random.split(key, 3)
    row_scale = jnp.exp(jax.random.uniform(key_rows, (TOKENS, 1), jnp.float32, math.log(0.3), math.log(3.0)))
    col_scale = jnp.exp(jax.random.uniform(key_cols, (1, D), jnp.float32, math.log(0.3), math.log(3.0)))
    value = jnp.clip(jax.random.normal(key_base, (TOKENS, D), jnp.float32), -4.0, 4.0)
    return (value * row_scale * col_scale).astype(jnp.bfloat16)


def draw_route_ids(key, part):
    key = jax.random.fold_in(key, 11)
    block_count = TOKENS // ROWS
    pair_count = ROWS * TOPK
    relabel = jax.random.permutation(jax.random.fold_in(key, 1), EXPERTS).astype(jnp.int32)

    def one_block(block_key):
        key_slots, key_order = jax.random.split(block_key)
        spare = jax.random.permutation(key_slots, (EXPERTS - 1) * CAP)[:pair_count - CAP].astype(jnp.int32)
        labels = jnp.concatenate([jnp.zeros((CAP,), jnp.int32), 1 + spare // CAP])
        labels = jnp.sort(labels)
        table = labels.reshape(TOPK, ROWS).T
        order = jax.random.permutation(key_order, ROWS)
        return table[order]
    block_keys = jax.random.split(jax.random.fold_in(key, 2), block_count)
    labels_all = jax.vmap(one_block)(block_keys).reshape(TOKENS, TOPK)
    return relabel[labels_all].astype(jnp.int32)


def steps_of(stream_key, dims, shards, smallest, top_value):
    loudness, own = 1.0, jax.random.fold_in(stream_key, 6)
    for axis_at, shards_of in shards:
        draws = jnp.exp(jax.random.uniform(jax.random.fold_in(own, axis_at), (shards_of,), jnp.float32, smallest / len(shards), top_value / len(shards)))
        loudness = loudness * jnp.repeat(draws, dims[axis_at] // shards_of).reshape([-1 if axis == axis_at else 1 for axis in range(len(dims))])
    return loudness


def centred(stream_key, extent, scale, bound, pieces=(), kind=jnp.bfloat16):
    array = scale * jax.random.normal(stream_key, extent, jnp.float32)
    if pieces:
        array = array * steps_of(stream_key, extent, pieces, -0.22, 0.18)
    return jnp.clip(array, -bound, bound).astype(kind)


def setup_inputs(seed: int = 0, part: int = 0) -> dict:
    arg_keys = jax.random.split(jax.random.key(seed), 10)
    own_keys = jax.random.split(jax.random.fold_in(arg_keys[9], part), 10)
    attn = centred(own_keys[0], (TOKENS, HEADS * HDIM), 1.0, 6.0, ((0, 8), (1, 4)))
    w_out = centred(arg_keys[1], (HEADS * HDIM, D), (HEADS * HDIM) ** -0.5, 0.0625, ((0, 4), (1, 8)))
    resid = draw_resid(jax.random.fold_in(jax.random.fold_in(arg_keys[9], part), 71), part)
    norm_gain = jnp.clip(1.0 + 0.18 * jax.random.normal(arg_keys[3], (D,), jnp.float32), 0.1, 1.9)
    route_ids = draw_route_ids(jax.random.fold_in(jax.random.fold_in(arg_keys[9], part), 71), part)
    gate_vals = jnp.clip(0.2 + 0.8 * jax.random.uniform(own_keys[5], (TOKENS, TOPK), jnp.float32) ** steps_of(own_keys[5], (TOKENS, TOPK), ((0, 32),), -0.2, 0.2), 0.2, 1.0)
    w_gate = centred(arg_keys[6], (EXPERTS, D, FF), D ** -0.5, 0.078125, ((0, 8), (2, 4)))
    w_up = centred(arg_keys[7], (EXPERTS, D, FF), D ** -0.5, 0.078125, ((0, 8), (2, 4)))
    w_down = centred(arg_keys[8], (EXPERTS, FF, D), FF ** -0.5, 0.15625, ((0, 8), (1, 4)))
    return dict(attn=attn, w_out=w_out, resid=resid, norm_gain=norm_gain, route_ids=route_ids, gate_vals=gate_vals, w_gate=w_gate, w_up=w_up, w_down=w_down)


def blocked_down(left_side, right_side):
    width_block = left_side.shape[1] // N_TENSOR
    down_sum = jnp.zeros((left_side.shape[0], right_side.shape[1]), jnp.float32)
    for quarter_idx in range(N_TENSOR):
        first_col = quarter_idx * width_block
        head_part = jnp.dot(left_side[:, first_col:first_col + width_block], right_side[first_col:first_col + width_block], preferred_element_type=jnp.float32)
        down_sum = down_sum + lax.optimization_barrier(head_part.astype(jnp.bfloat16)).astype(jnp.float32)
    return down_sum

def reference(attn, w_out, resid, norm_gain, route_ids, gate_vals, w_gate, w_up, w_down):
    hidden = resid.astype(jnp.float32) + blocked_down(attn, w_out)
    scale_inv = lax.rsqrt(lax.optimization_barrier(jnp.mean(hidden * hidden, axis=1, keepdims=True)) + 1e-06)
    normed = (hidden * scale_inv * norm_gain).astype(jnp.bfloat16)
    pair_ids = route_ids.reshape(-1)
    pair_gates = gate_vals.reshape(-1)
    slot_total = N_EXPERT * N_TENSOR * CAP
    top_count = route_ids.shape[1]

    def one_expert(mixture, inputs):
        expert_index, gate_matrix, up_matrix, down_matrix = inputs
        matched = pair_ids == expert_index
        chosen = jnp.nonzero(matched, size=slot_total, fill_value=0)[0].astype(jnp.int32)
        live = jnp.arange(slot_total, dtype=jnp.int32) < jnp.sum(matched.astype(jnp.int32))
        token_rows = chosen // top_count
        gathered = normed[token_rows]
        gate_act = jnp.dot(gathered, gate_matrix, preferred_element_type=jnp.float32)
        up_act = jnp.dot(gathered, up_matrix, preferred_element_type=jnp.float32)
        activation = (jax.nn.silu(gate_act) * up_act).astype(jnp.bfloat16)
        expert_out = blocked_down(activation, down_matrix)
        weight = jnp.where(live, pair_gates[chosen], 0.0)
        return (mixture.at[token_rows].add(expert_out * weight[:, None]), None)
    mixture, unused = lax.scan(one_expert, jnp.zeros(hidden.shape, jnp.float32), (jnp.arange(EXPERTS, dtype=jnp.int32), w_gate, w_up, w_down))
    return (hidden + mixture).astype(jnp.bfloat16)
```

```python
import functools

import jax
import jax.numpy as jnp
from jax import lax
from jax.experimental import pallas as pl
from jax.experimental.pallas import tpu as pltpu
from jax.sharding import PartitionSpec as P

MESH = pl.DeviceIdType.MESH
BF = jnp.bfloat16
F32 = jnp.float32

QN = 320
DN = 2048 - 4 * QN
WIDTHS = (256, 256, 128)
OFFS = (0, 256, 512)
STRIP = 640


class Place:
    def __init__(self):
        self.z = lax.axis_index("dp")
        self.e = lax.axis_index("expert")
        self.x = lax.axis_index("tensor")
        self.y = self.e // 2
        self.c = self.e % 2

    def at(self, dx=0, dy=0, dz=0, flip=False):
        core = 1 - self.c if flip else self.c
        return (
            lax.rem(self.z + dz, 4),
            lax.rem(self.y + dy, 4) * 2 + core,
            lax.rem(self.x + dx, 4),
        )


class Links:
    def __init__(self, send_sems, recv_sems):
        self.send_sems, self.recv_sems, self.open = send_sems, recv_sems, []

    def send(self, src, dst, device):
        i = len(self.open)
        copy = pltpu.make_async_remote_copy(
            src_ref=src,
            dst_ref=dst,
            send_sem=self.send_sems.at[i],
            recv_sem=self.recv_sems.at[i],
            device_id=device,
            device_id_type=MESH,
        )
        copy.start()
        self.open.append(copy)
        return copy

    def drain(self):
        for copy in self.open:
            copy.wait_send()


def greet(devices):
    barrier = pltpu.get_barrier_semaphore()
    for device in devices:
        pl.semaphore_signal(barrier, inc=1, device_id=device, device_id_type=MESH)
    pl.semaphore_wait(barrier, len(devices))


A_SENDS = 96


def project(
    attn, w_out, resid, gain, hid_out,
    a_buf, w_own, w0, w1, w2, res, hid,
    p_own, p0, p1, p2, l_own, l0, l1, l2, f_own, f0, f1, f2,
    ssq, ssq_sib, send_sems, recv_sems, local_sems,
):
    me = Place()
    z, x, y, c = me.z, me.x, me.y, me.c
    w = (w0, w1, w2)
    parts = (p0, p1, p2)
    relays = (l0, l1, l2)
    finals = (f0, f1, f2)
    sib = me.at(flip=True)
    xp, xm, xo = me.at(dx=1), me.at(dx=3), me.at(dx=2)
    yp, ym, zp, zm = me.at(dy=1), me.at(dy=3), me.at(dz=1), me.at(dz=3)
    links = Links(send_sems, recv_sems)

    load_w = pltpu.make_async_copy(w_out, w_own, local_sems.at[0])
    load_w.start()
    load_a = pltpu.make_async_copy(attn, a_buf.at[c], local_sems.at[1])
    load_a.start()
    load_r = []
    for b in range(4):
        col = pl.multiple_of((2 * b + c) * STRIP, 128)
        load = pltpu.make_async_copy(
            resid.at[:, pl.ds(col, STRIP)], res.at[c, :, pl.ds(b * STRIP, STRIP)], local_sems.at[2 + b]
        )
        load.start()
        load_r.append(load)

    greet([sib, yp, ym, zp, zm, xp, xm])

    def rows_q(half=None):
        start = z * QN
        if half is None:
            return pl.ds(pl.multiple_of(start, 16), QN)
        return pl.ds(pl.multiple_of(start + half * (QN // 2), 16), QN // 2)

    rows_d = pl.ds(4 * QN, DN)

    def rows_dh(half):
        return pl.ds(4 * QN + half * (DN // 2), DN // 2)

    def own(j, rows):
        return w_out.at[rows, pl.ds(OFFS[j], WIDTHS[j])]

    def send_q(j):
        return (
            links.send(own(j, rows_q()), w[j].at[2, rows_q()], yp),
            links.send(own(j, rows_q()), w[j].at[0, rows_q()], ym),
        )

    def send_d(j):
        return (
            links.send(own(j, rows_d), w[j].at[2, rows_d], yp),
            links.send(own(j, rows_d), w[j].at[0, rows_d], ym),
        )

    n = len(WIDTHS)
    q, d, rq, rd, zs, zo, zr = {}, {}, {}, {}, {}, {}, {}
    q[0] = send_q(0)
    sib_a = links.send(attn, a_buf.at[c], sib)
    d[0] = send_d(0)
    sib_r = []
    for b in range(4):
        col = pl.multiple_of((2 * b + 1 - c) * STRIP, 128)
        sib_r.append(
            links.send(resid.at[:, pl.ds(col, STRIP)], res.at[c, :, pl.ds(b * STRIP, STRIP)], sib)
        )

    def multiply(block, part, core, col, width):
        def step(m, carry):
            rows = pl.ds(pl.multiple_of(m * 256, 256), 256)
            out = jnp.dot(a_buf[core, rows, :], block[...], preferred_element_type=F32).astype(BF)
            part[2 * m, core, :, pl.ds(col, width)] = out[:128]
            part[2 * m + 1, core, :, pl.ds(col, width)] = out[128:]
            return carry

        lax.fori_loop(0, 2, step, 0)

    ahead, behind, over = lax.rem(x + 1, 4), lax.rem(x + 3, 4), lax.rem(x + 2, 4)

    def reduce_first(part, relay, final):
        return (
            links.send(part.at[over, 0], relay.at[0], xp),
            links.send(part.at[over, 1], relay.at[1], xm),
            links.send(part.at[ahead, 1], final.at[0, 1], xp),
            links.send(part.at[behind, 0], final.at[1, 0], xm),
        )

    def reduce_second(first, part, relay, final):
        first[0].wait_recv()
        part[ahead, 0] = (part[ahead, 0].astype(F32) + relay[0].astype(F32)).astype(BF)
        one = links.send(part.at[ahead, 0], final.at[0, 0], xp)
        first[1].wait_recv()
        part[behind, 1] = (part[behind, 1].astype(F32) + relay[1].astype(F32)).astype(BF)
        two = links.send(part.at[behind, 1], final.at[1, 1], xm)
        return (first[2], first[3], one, two)

    def on_q(j):
        q[j][0].wait_recv()
        one = links.send(w[j].at[2, rows_q(0)], w[j].at[1, rows_q(0)], yp)
        z_a = (
            links.send(w[j].at[2, rows_q()], w[j].at[2, rows_q()], zp),
            links.send(w[j].at[2, rows_q()], w[j].at[2, rows_q()], zm),
        )
        q[j][1].wait_recv()
        two = links.send(w[j].at[0, rows_q(1)], w[j].at[1, rows_q(1)], ym)
        z_b = (
            links.send(w[j].at[0, rows_q()], w[j].at[0, rows_q()], zp),
            links.send(w[j].at[0, rows_q()], w[j].at[0, rows_q()], zm),
        )
        rq[j] = (one, two)
        zs[j] = (z_a, z_b)
        if j + 1 < n:
            q[j + 1] = send_q(j + 1)

    def on_rq(j):
        rq[j][0].wait_recv()
        rq[j][1].wait_recv()
        zo[j] = (
            links.send(w[j].at[1, rows_q()], w[j].at[1, rows_q()], zp),
            links.send(w[j].at[1, rows_q()], w[j].at[1, rows_q()], zm),
        )

    def on_d(j):
        d[j][0].wait_recv()
        one = links.send(w[j].at[2, rows_dh(0)], w[j].at[1, rows_dh(0)], yp)
        d[j][1].wait_recv()
        two = links.send(w[j].at[0, rows_dh(1)], w[j].at[1, rows_dh(1)], ym)
        rd[j] = (one, two)
        if j + 1 < n:
            d[j + 1] = send_d(j + 1)

    def z_relay(j, pair, slot):
        low = pl.ds(pl.multiple_of(lax.rem(z + 3, 4) * QN, 16), QN // 2)
        high = pl.ds(pl.multiple_of(lax.rem(z + 1, 4) * QN + QN // 2, 16), QN // 2)
        pair[0].wait_recv()
        one = links.send(w[j].at[slot, low], w[j].at[slot, low], zp)
        pair[1].wait_recv()
        two = links.send(w[j].at[slot, high], w[j].at[slot, high], zm)
        zr.setdefault(j, []).extend((one, two))

    def on_z(j):
        z_relay(j, zs[j][0], 2)
        z_relay(j, zs[j][1], 0)

    def on_zo(j):
        z_relay(j, zo[j], 1)

    def all_in(j):
        for copy in rd[j]:
            copy.wait_recv()
        for copy in zr[j]:
            copy.wait_recv()

    def compute(j):
        for slot in range(3):
            for core in range(2):
                multiply(w[j].at[slot], parts[j], core, slot * WIDTHS[j], WIDTHS[j])
        return reduce_first(parts[j], relays[j], finals[j])

    first, second = {}, {}
    load_w.wait()
    load_a.wait()
    multiply(w_own, p_own, c, 0, STRIP)
    sib_a.wait_recv()
    multiply(w_own, p_own, 1 - c, 0, STRIP)
    first["own"] = reduce_first(p_own, l_own, f_own)
    on_q(0)
    second["own"] = reduce_second(first["own"], p_own, l_own, f_own)

    def finish(group, part, final, strips, width):
        for copy in second[group]:
            copy.wait_recv()
        for k, (col, strip) in enumerate(strips):
            cols = pl.ds(col, width)
            for core in range(2):
                at = pl.ds(k * width, width)
                total = (
                    res[core, :, cols].astype(F32)
                    + part[x, core, :, at].astype(F32)
                    + final[0, core, :, at].astype(F32)
                    + final[1, core, :, at].astype(F32)
                )
                hid[core, :, cols] = total
                add = jnp.sum(total * total, axis=1, keepdims=True)
                ssq[core] = ssq[core] + jnp.broadcast_to(add, (128, 128))

    ssq[...] = jnp.zeros_like(ssq)

    def strips_of(j):
        return [
            (pl.multiple_of(lax.rem(y + 1 + slot, 4) * STRIP + OFFS[j], 128), slot)
            for slot in range(3)
        ]

    on_rq(0)
    for j in range(n):
        on_d(j)
        on_z(j)
        on_zo(j)
        if j + 1 < n:
            on_q(j + 1)
        if j == 0:
            for load in load_r:
                load.wait()
            for copy in sib_r:
                copy.wait_recv()
            finish("own", p_own, f_own, [(pl.multiple_of(y * STRIP, 128), 0)], STRIP)
        else:
            second[j - 1] = reduce_second(first[j - 1], parts[j - 1], relays[j - 1], finals[j - 1])
        all_in(j)
        first[j] = compute(j)
        if j + 1 < n:
            on_rq(j + 1)
        if j > 0:
            finish(j - 1, parts[j - 1], finals[j - 1], strips_of(j - 1), WIDTHS[j - 1])
    last = n - 1
    second[last] = reduce_second(first[last], parts[last], relays[last], finals[last])
    finish(last, parts[last], finals[last], strips_of(last), WIDTHS[last])

    back = links.send(hid.at[1 - c], hid_out.at[c], sib)
    keep = pltpu.make_async_copy(hid.at[c], hid_out.at[c], local_sems.at[6])
    keep.start()
    back.wait_recv()
    keep.wait()
    links.drain()


def scratch_a():
    def triple(shape):
        return [pltpu.VMEM(shape(STRIP), BF)] + [pltpu.VMEM(shape(3 * v), BF) for v in WIDTHS]

    return [
        pltpu.VMEM((2, 512, 2048), BF),
        pltpu.VMEM((2048, STRIP), BF),
        *[pltpu.VMEM((3, 2048, v), BF) for v in WIDTHS],
        pltpu.VMEM((2, 128, 4 * STRIP), BF),
        pltpu.VMEM((2, 128, 4 * STRIP), F32),
        *triple(lambda v: (4, 2, 128, v)),
        *triple(lambda v: (2, 128, v)),
        *triple(lambda v: (2, 2, 128, v)),
        pltpu.VMEM((2, 128, 128), F32),
        pltpu.VMEM((2, 128, 128), F32),
        pltpu.SemaphoreType.DMA((A_SENDS,)),
        pltpu.SemaphoreType.DMA((A_SENDS,)),
        pltpu.SemaphoreType.DMA((8,)),
    ]


ANY = pl.BlockSpec(memory_space=pl.ANY)
VM = pl.BlockSpec(memory_space=pltpu.VMEM)


def call_a(attn, w_out, resid, gain):
    return pl.pallas_call(
        project,
        out_shape=jax.ShapeDtypeStruct((2, 128, 4 * STRIP), F32),
        in_specs=[ANY, ANY, ANY, VM],
        out_specs=ANY,
        scratch_shapes=scratch_a(),
        compiler_params=pltpu.CompilerParams(
            collective_id=0, has_side_effects=True, vmem_limit_bytes=56 * 2**20
        ),
        name="project",
    )(attn, w_out, resid, gain)


def expert_rows(received, w_gate, w_up, w_down):
    layout = received.shape
    flat_rows = received.reshape(-1, layout[-1])
    gate_act = jnp.dot(flat_rows, w_gate[0], preferred_element_type=F32)
    up_act = jnp.dot(flat_rows, w_up[0], preferred_element_type=F32)
    activation = (jax.nn.silu(gate_act) * up_act).astype(BF)
    down_part = jnp.dot(activation, w_down[0], preferred_element_type=F32).astype(BF)
    return down_part.reshape(layout)


def shards(attn, w_out, resid, norm_gain, route_ids, gate_vals, w_gate, w_up, w_down):
    row_count = resid.shape[0]
    width_model = resid.shape[1]
    top_count = route_ids.shape[1]
    expert_count = lax.axis_size("expert")
    group_width = lax.axis_size("tensor")
    capacity = min(row_count, 3 * row_count * top_count // (2 * expert_count))
    halves = call_a(attn, w_out, resid, norm_gain.reshape(1, -1))
    hidden = halves.reshape(2, 128, 4, STRIP).transpose(1, 2, 0, 3).reshape(128, width_model)
    scale_inv = lax.rsqrt(jnp.mean(hidden * hidden, axis=1, keepdims=True) + 1e-06)
    normed = (hidden * scale_inv * norm_gain).astype(jnp.bfloat16)
    pair_ids = route_ids.reshape(-1)
    one_hot = (pair_ids[:, None] == jnp.arange(expert_count, dtype=jnp.int32)[None, :]).astype(
        jnp.int32
    )
    earlier = jnp.cumsum(one_hot, axis=0) - one_hot
    slot_index = jnp.sum(earlier * one_hot, axis=1)
    target = pair_ids * capacity + slot_index
    placed = (
        jnp.arange(expert_count * capacity, dtype=jnp.int32)[:, None] == target[None, :]
    ).astype(jnp.float32)
    placed_rows = placed.reshape(expert_count * capacity, row_count, top_count)
    dispatch = jnp.sum(placed_rows, axis=2)
    weights_comb = jnp.sum(placed_rows * gate_vals[None, :, :], axis=2)
    send_rows = jnp.dot(
        dispatch.astype(jnp.bfloat16), normed, preferred_element_type=jnp.float32
    ).astype(jnp.bfloat16)
    send_rows = send_rows.reshape(expert_count, capacity, width_model)
    copies = jnp.broadcast_to(
        send_rows[:, None], (expert_count, group_width, capacity, width_model)
    )
    copies = copies.reshape(expert_count * group_width, capacity, width_model)
    returned = lax.all_to_all(
        expert_rows(
            lax.all_to_all(copies, ("expert", "tensor"), split_axis=0, concat_axis=0, tiled=True),
            w_gate,
            w_up,
            w_down,
        ),
        ("expert", "tensor"),
        split_axis=0,
        concat_axis=0,
        tiled=True,
    )
    quarters = jnp.sum(
        returned.reshape(expert_count, group_width, capacity, width_model),
        axis=1,
        dtype=jnp.float32,
    )
    mixture = jnp.dot(
        weights_comb.T,
        quarters.reshape(expert_count * capacity, width_model),
        precision=lax.Precision.HIGHEST,
        preferred_element_type=jnp.float32,
    )
    return (hidden + mixture).astype(jnp.bfloat16)


def solution(mesh):
    placed = (
        P(("dp", "expert"), "tensor"),
        P("tensor", "expert"),
        P(("dp", "expert", "tensor"), None),
        P(),
        P(("dp", "expert", "tensor"), None),
        P(("dp", "expert", "tensor"), None),
        P("expert", None, "tensor"),
        P("expert", None, "tensor"),
        P("expert", "tensor", None),
    )
    return jax.shard_map(
        shards,
        mesh=mesh,
        in_specs=placed,
        out_specs=P(("dp", "expert", "tensor"), None),
        check_vma=False,
    )
```

```python
import functools

import jax
import jax.numpy as jnp
from jax import lax
from jax.experimental import pallas as pl
from jax.experimental.pallas import tpu as pltpu
from jax.sharding import PartitionSpec as P

MESH = pl.DeviceIdType.MESH
BF = jnp.bfloat16
F32 = jnp.float32

QN = 320
DN = 2048 - 4 * QN
WIDTHS = (256, 256, 128)
OFFS = (0, 256, 512)
STRIP = 640


class Place:
    def __init__(self):
        self.z = lax.axis_index("dp")
        self.e = lax.axis_index("expert")
        self.x = lax.axis_index("tensor")
        self.y = self.e // 2
        self.c = self.e % 2

    def at(self, dx=0, dy=0, dz=0, flip=False):
        core = 1 - self.c if flip else self.c
        return (
            lax.rem(self.z + dz, 4),
            lax.rem(self.y + dy, 4) * 2 + core,
            lax.rem(self.x + dx, 4),
        )


class Links:
    def __init__(self, send_sems, recv_sems):
        self.send_sems, self.recv_sems, self.open = send_sems, recv_sems, []

    def send(self, src, dst, device):
        i = len(self.open)
        copy = pltpu.make_async_remote_copy(
            src_ref=src,
            dst_ref=dst,
            send_sem=self.send_sems.at[i],
            recv_sem=self.recv_sems.at[i],
            device_id=device,
            device_id_type=MESH,
        )
        copy.start()
        self.open.append(copy)
        return copy

    def send_both(self, sources, dst, devices, core):
        i = len(self.open)
        copies = [
            pltpu.make_async_remote_copy(
                src_ref=sources[k],
                dst_ref=dst,
                send_sem=self.send_sems.at[i + k],
                recv_sem=self.recv_sems.at[i + core],
                device_id=devices[k],
                device_id_type=MESH,
            )
            for k in range(2)
        ]
        for copy in copies:
            copy.start()
        self.open.extend(copies)
        return [
            pltpu.make_async_remote_copy(
                src_ref=sources[k],
                dst_ref=dst,
                send_sem=self.send_sems.at[i + k],
                recv_sem=self.recv_sems.at[i + k],
                device_id=devices[k],
                device_id_type=MESH,
            )
            for k in range(2)
        ]

    def drain(self):
        for copy in self.open:
            copy.wait_send()


def greet(devices):
    barrier = pltpu.get_barrier_semaphore()
    for device in devices:
        pl.semaphore_signal(barrier, inc=1, device_id=device, device_id_type=MESH)
    pl.semaphore_wait(barrier, len(devices))


SENDS = 176
CAP = 24
PAIR = 2 * CAP
ORDER = (0, 3, 1, 2)


def layer(
    attn, w_out, resid, gain, codes, gates, w_gate, w_up, w_down, out,
    a_buf, w_own, w0, w1, w2, res, hid,
    p_own, p0, p1, p2, l_own, l0, l1, l2, f_own, f0, f1, f2,
    ssq, ssq_sib, code, gate, w_gu, w_dn, sent, rows_in, act, done, back, comb, fin,
    send_sems, recv_sems, local_sems,
):
    me = Place()
    z, x, y, c = me.z, me.x, me.y, me.c
    w = (w0, w1, w2)
    parts = (p0, p1, p2)
    relays = (l0, l1, l2)
    finals = (f0, f1, f2)
    sib = me.at(flip=True)
    xp, xm, xo = me.at(dx=1), me.at(dx=3), me.at(dx=2)
    yp, ym, zp, zm = me.at(dy=1), me.at(dy=3), me.at(dz=1), me.at(dz=3)
    links = Links(send_sems, recv_sems)

    load_w = pltpu.make_async_copy(w_out, w_own, local_sems.at[0])
    load_w.start()
    load_a = pltpu.make_async_copy(attn, a_buf.at[c], local_sems.at[1])
    load_a.start()
    load_r = []
    for b in range(4):
        col = pl.multiple_of((2 * b + c) * STRIP, 128)
        load = pltpu.make_async_copy(
            resid.at[:, pl.ds(col, STRIP)], res.at[c, :, pl.ds(b * STRIP, STRIP)], local_sems.at[2 + b]
        )
        load.start()
        load_r.append(load)

    loads = []
    for half in range(2):
        for b in range(4):
            source = pl.ds((2 * b + half) * STRIP, STRIP)
            target = pl.ds(b * STRIP, STRIP)
            for k, weight in enumerate((w_gate, w_up)):
                loads.append((weight.at[0, source], w_gu.at[half, target, pl.ds(k * 384, 384)]))
    quarter = pl.ds(pl.multiple_of(x * 1280, 128), 1280)
    loads.append((w_down.at[0, :, quarter], w_dn.at[pl.ds(0, 384)]))
    loads.append((codes, code.at[0, c]))
    loads.append((gates, gate.at[c]))
    loads = [
        pltpu.make_async_copy(source, target, local_sems.at[7 + k])
        for k, (source, target) in enumerate(loads)
    ]

    def chip(dy):
        return [(z, lax.rem(y + dy, 4) * 2 + core, x) for core in range(2)]

    zo_, xs = me.at(dz=2), (None, xp, xo, xm)
    greet([sib, *chip(1), *chip(2), *chip(3), zp, zm, zo_, xp, xm, xo])
    for load in loads:
        load.start()

    def rows_q(half=None):
        start = z * QN
        if half is None:
            return pl.ds(pl.multiple_of(start, 16), QN)
        return pl.ds(pl.multiple_of(start + half * (QN // 2), 16), QN // 2)

    rows_d = pl.ds(4 * QN, DN)

    def rows_dh(half):
        return pl.ds(4 * QN + half * (DN // 2), DN // 2)

    def own(j, rows):
        return w_out.at[rows, pl.ds(OFFS[j], WIDTHS[j])]

    def send_q(j):
        return (
            links.send(own(j, rows_q()), w[j].at[2, rows_q()], yp),
            links.send(own(j, rows_q()), w[j].at[0, rows_q()], ym),
        )

    def send_d(j):
        return (
            links.send(own(j, rows_d), w[j].at[2, rows_d], yp),
            links.send(own(j, rows_d), w[j].at[0, rows_d], ym),
        )

    n = len(WIDTHS)
    q, d, rq, rd, zs, zo, zr = {}, {}, {}, {}, {}, {}, {}
    q[0] = send_q(0)
    sib_a = links.send(attn, a_buf.at[c], sib)
    d[0] = send_d(0)
    sib_r = []
    for b in range(4):
        col = pl.multiple_of((2 * b + 1 - c) * STRIP, 128)
        sib_r.append(
            links.send(resid.at[:, pl.ds(col, STRIP)], res.at[c, :, pl.ds(b * STRIP, STRIP)], sib)
        )

    sib_code = links.send(codes, code.at[0, c], sib)
    sib_gate = links.send(gates, gate.at[c], sib)
    dn_rows = pl.multiple_of(z * 96, 16)
    dn_x = {}
    for dx in (1, 3, 2):
        column = pl.multiple_of(lax.rem(x + dx, 4) * 1280, 128)
        dn_x[4 - dx] = links.send(
            w_down.at[0, pl.ds(dn_rows, 96), pl.ds(column, 1280)],
            w_dn.at[pl.ds((4 - dx) * 384 + dn_rows, 96)],
            xs[dx],
        )

    def multiply(block, part, core, col, width):
        def step(m, carry):
            rows = pl.ds(pl.multiple_of(m * 256, 256), 256)
            out = jnp.dot(a_buf[core, rows, :], block[...], preferred_element_type=F32).astype(BF)
            part[2 * m, core, :, pl.ds(col, width)] = out[:128]
            part[2 * m + 1, core, :, pl.ds(col, width)] = out[128:]
            return carry

        lax.fori_loop(0, 2, step, 0)

    ahead, behind, over = lax.rem(x + 1, 4), lax.rem(x + 3, 4), lax.rem(x + 2, 4)

    def reduce_first(part, relay, final):
        return (
            links.send(part.at[over, 0], relay.at[0], xp),
            links.send(part.at[over, 1], relay.at[1], xm),
            links.send(part.at[ahead, 1], final.at[0, 1], xp),
            links.send(part.at[behind, 0], final.at[1, 0], xm),
        )

    def reduce_second(first, part, relay, final):
        first[0].wait_recv()
        part[ahead, 0] = (part[ahead, 0].astype(F32) + relay[0].astype(F32)).astype(BF)
        one = links.send(part.at[ahead, 0], final.at[0, 0], xp)
        first[1].wait_recv()
        part[behind, 1] = (part[behind, 1].astype(F32) + relay[1].astype(F32)).astype(BF)
        two = links.send(part.at[behind, 1], final.at[1, 1], xm)
        return (first[2], first[3], one, two)

    def on_q(j):
        q[j][0].wait_recv()
        one = links.send(w[j].at[2, rows_q(0)], w[j].at[1, rows_q(0)], yp)
        z_a = (
            links.send(w[j].at[2, rows_q()], w[j].at[2, rows_q()], zp),
            links.send(w[j].at[2, rows_q()], w[j].at[2, rows_q()], zm),
        )
        q[j][1].wait_recv()
        two = links.send(w[j].at[0, rows_q(1)], w[j].at[1, rows_q(1)], ym)
        z_b = (
            links.send(w[j].at[0, rows_q()], w[j].at[0, rows_q()], zp),
            links.send(w[j].at[0, rows_q()], w[j].at[0, rows_q()], zm),
        )
        rq[j] = (one, two)
        zs[j] = (z_a, z_b)
        if j + 1 < n:
            q[j + 1] = send_q(j + 1)

    def on_rq(j):
        rq[j][0].wait_recv()
        rq[j][1].wait_recv()
        zo[j] = (
            links.send(w[j].at[1, rows_q()], w[j].at[1, rows_q()], zp),
            links.send(w[j].at[1, rows_q()], w[j].at[1, rows_q()], zm),
        )

    def on_d(j):
        d[j][0].wait_recv()
        one = links.send(w[j].at[2, rows_dh(0)], w[j].at[1, rows_dh(0)], yp)
        d[j][1].wait_recv()
        two = links.send(w[j].at[0, rows_dh(1)], w[j].at[1, rows_dh(1)], ym)
        rd[j] = (one, two)
        if j + 1 < n:
            d[j + 1] = send_d(j + 1)

    def z_relay(j, pair, slot):
        low = pl.ds(pl.multiple_of(lax.rem(z + 3, 4) * QN, 16), QN // 2)
        high = pl.ds(pl.multiple_of(lax.rem(z + 1, 4) * QN + QN // 2, 16), QN // 2)
        pair[0].wait_recv()
        one = links.send(w[j].at[slot, low], w[j].at[slot, low], zp)
        pair[1].wait_recv()
        two = links.send(w[j].at[slot, high], w[j].at[slot, high], zm)
        zr.setdefault(j, []).extend((one, two))

    def on_z(j):
        z_relay(j, zs[j][0], 2)
        z_relay(j, zs[j][1], 0)

    def on_zo(j):
        z_relay(j, zo[j], 1)

    def all_in(j):
        for copy in rd[j]:
            copy.wait_recv()
        for copy in zr[j]:
            copy.wait_recv()

    def compute(j):
        for slot in range(3):
            for core in range(2):
                multiply(w[j].at[slot], parts[j], core, slot * WIDTHS[j], WIDTHS[j])
        return reduce_first(parts[j], relays[j], finals[j])

    first, second = {}, {}
    load_w.wait()
    load_a.wait()
    multiply(w_own, p_own, c, 0, STRIP)
    sib_a.wait_recv()
    multiply(w_own, p_own, 1 - c, 0, STRIP)
    first["own"] = reduce_first(p_own, l_own, f_own)
    loads[-2].wait()
    sib_code.wait_recv()
    code_x = {4 - dx: links.send(code.at[0], code.at[4 - dx], xs[dx]) for dx in (1, 3, 2)}
    on_q(0)
    second["own"] = reduce_second(first["own"], p_own, l_own, f_own)

    def finish(group, part, final, strips, width):
        for copy in second[group]:
            copy.wait_recv()
        for k, (col, strip) in enumerate(strips):
            cols = pl.ds(col, width)
            for core in range(2):
                at = pl.ds(k * width, width)
                total = (
                    res[core, :, cols].astype(F32)
                    + part[x, core, :, at].astype(F32)
                    + final[0, core, :, at].astype(F32)
                    + final[1, core, :, at].astype(F32)
                )
                hid[core, :, cols] = total
                add = jnp.sum(total * total, axis=1, keepdims=True)
                ssq[core] = ssq[core] + jnp.broadcast_to(add, (128, 128))

    ssq[...] = jnp.zeros_like(ssq)

    def strips_of(j):
        return [
            (pl.multiple_of(lax.rem(y + 1 + slot, 4) * STRIP + OFFS[j], 128), slot)
            for slot in range(3)
        ]

    on_rq(0)
    for j in range(n):
        on_d(j)
        on_z(j)
        on_zo(j)
        if j + 1 < n:
            on_q(j + 1)
        if j == 0:
            for load in load_r:
                load.wait()
            for copy in sib_r:
                copy.wait_recv()
            finish("own", p_own, f_own, [(pl.multiple_of(y * STRIP, 128), 0)], STRIP)
        else:
            second[j - 1] = reduce_second(first[j - 1], parts[j - 1], relays[j - 1], finals[j - 1])
        if j == n - 1:
            dn_z = []
            for slot in (3, 1, 2):
                dn_x[slot].wait_recv()
                piece = w_dn.at[pl.ds(slot * 384 + dn_rows, 96)]
                dn_z.extend(links.send(piece, piece, device) for device in (zp, zm, zo_))
        all_in(j)
        first[j] = compute(j)
        if j + 1 < n:
            on_rq(j + 1)
        if j > 0:
            finish(j - 1, parts[j - 1], finals[j - 1], strips_of(j - 1), WIDTHS[j - 1])
    last = n - 1
    second[last] = reduce_second(first[last], parts[last], relays[last], finals[last])
    finish(last, parts[last], finals[last], strips_of(last), WIDTHS[last])

    share = links.send(ssq, ssq_sib, sib)

    def pick(slot, chips):
        blocks = []
        for dy in chips:
            base = lax.rem(y + dy, 4) * (2 * PAIR)
            place = base + lax.broadcasted_iota(jnp.int32, (2 * PAIR, 128), 0)
            blocks.append(
                jnp.concatenate(
                    [
                        (place == code[slot, core, 0:1, :]).astype(F32).astype(BF)
                        for core in range(2)
                    ],
                    axis=1,
                )
            )
        return blocks[0] if len(blocks) == 1 else jnp.concatenate(blocks, axis=0)

    loads[-1].wait()
    sib_gate.wait_recv()
    share.wait_recv()
    for core in range(2):
        scale = lax.rsqrt((ssq[core] + ssq_sib[core])[:, 0:1] / 5120.0 + 1e-06)
        for b in range(4):
            cols = pl.ds(b * STRIP, STRIP)
            col = pl.multiple_of((2 * b + c) * STRIP, 128)
            res[core, :, cols] = (hid[core, :, cols] * scale * gain[0:1, pl.ds(col, STRIP)]).astype(BF)

    arrive = {}

    def dispatch(dy):
        choice = pick(0, (dy,))
        for b in range(4):
            cols = pl.ds(b * STRIP, STRIP)
            normed = res[:, :, cols].reshape(256, STRIP)
            rows = jnp.dot(choice, normed, preferred_element_type=F32).astype(BF)
            sent[dy, :, :, cols] = rows.reshape(2, PAIR, STRIP)
        slot = (4 - dy) % 4
        if dy == 0:
            arrive[0] = [links.send(sent.at[0, 1 - c], rows_in.at[0, 0, c], sib)]
            rows_in[0, 0, c] = sent[0, c]
        else:
            arrive[slot] = links.send_both(
                [sent.at[dy, 0], sent.at[dy, 1]], rows_in.at[slot, 0, c], chip(dy), c
            )

    spread, relay_x = {}, {}

    def spread_rows(r):
        for copy in arrive[r]:
            copy.wait_recv()
        spread[r] = (
            links.send(rows_in.at[r, 0], rows_in.at[r, 3], xp),
            links.send(rows_in.at[r, 0], rows_in.at[r, 1], xm),
        )

    def relay_rows(r):
        spread[r][0].wait_recv()
        one = links.send(rows_in.at[r, 3, 0], rows_in.at[r, 2, 0], xp)
        spread[r][1].wait_recv()
        two = links.send(rows_in.at[r, 1, 1], rows_in.at[r, 2, 1], xm)
        relay_x[r] = (one, two)

    act_x = {}

    def gate_up(r):
        for copy in relay_x[r]:
            copy.wait_recv()
        both = jnp.dot(
            rows_in[r, :, 0].reshape(4 * PAIR, 4 * STRIP), w_gu[0], preferred_element_type=F32
        ) + jnp.dot(
            rows_in[r, :, 1].reshape(4 * PAIR, 4 * STRIP), w_gu[1], preferred_element_type=F32
        )
        left, right = both[:, :384], both[:, 384:]
        made = (left / (1.0 + jnp.exp(-left)) * right).astype(BF).reshape(4, PAIR, 384)
        for slot in range(4):
            act[r, lax.rem(x + slot, 4), :, pl.ds(0, 384)] = made[slot]
        mine = act.at[r, :, :, pl.ds(0, 384)]
        act_x[r] = [
            links.send(mine, act.at[r, :, :, pl.ds((4 - dx) * 384, 384)], xs[dx]) for dx in (2, 1, 3)
        ]

    home = {}

    def down(r, final):
        for copy in act_x[r]:
            copy.wait_recv()
        whole = jnp.dot(
            act[r].reshape(4 * PAIR, 1536), w_dn[...], preferred_element_type=F32
        ).astype(BF).reshape(4, PAIR, 1280)
        for core in range(2):
            done[r, core] = whole[:, :, core * STRIP:(core + 1) * STRIP]
        slot = (4 - r) % 4
        if r == 0:
            home[0] = [links.send(done.at[0, 1 - c], back.at[0, c], sib)]
            back[0, c] = done[0, c]
        elif not final:
            home[slot] = links.send_both([done.at[r, 0], done.at[r, 1]], back.at[slot, c], chip(r), c)
        else:
            home[slot] = []
            for dx in (2, 1, 3, 0):
                t = lax.rem(x + dx, 4)
                home[slot].append(
                    links.send_both(
                        [done.at[r, 0, t], done.at[r, 1, t]], back.at[slot, c, t], chip(r), c
                    )
                )

    for dy in (0, 1, 3, 2):
        dispatch(dy)
        if dy == 0:
            spread_rows(0)
    for load in loads[:-2]:
        load.wait()
    for slot in (1, 2, 3):
        code_x[slot].wait_recv()
    spread_rows(ORDER[1])
    for k, r in enumerate(ORDER):
        relay_rows(r)
        if k + 2 < 4:
            spread_rows(ORDER[k + 2])
        gate_up(r)
        if k == 1:
            for copy in dn_z:
                copy.wait_recv()
        if k > 0:
            down(ORDER[k - 1], False)
    down(ORDER[3], True)

    ending = (4 - ORDER[3]) % 4
    for slot in range(4):
        if slot != ending:
            for copy in home[slot]:
                copy.wait_recv()
    over_x = {}
    for k, dx in enumerate((2, 1, 3, 0)):
        for copy in home[ending][k]:
            copy.wait_recv()
        t = lax.rem(x + dx, 4)
        mixed = lax.dot_general(
            pick(dx, (0, 1, 2, 3)),
            back[:, :, t].reshape(8 * PAIR, STRIP),
            (((0,), (0,)), ((), ())),
            preferred_element_type=F32,
        ).astype(BF)
        if dx == 0:
            fin[0] = mixed
        else:
            comb[dx] = mixed
            over_x[4 - dx] = links.send(comb.at[dx], fin.at[4 - dx], xs[dx])

    leave, stay = [], []
    for slot in (0, 1, 3, 2):
        if slot:
            over_x[slot].wait_recv()
        b = lax.rem(x + slot, 4)
        cols = pl.ds(pl.multiple_of(b * STRIP, 128), STRIP)
        col = pl.ds(pl.multiple_of((2 * b + c) * STRIP, 128), STRIP)
        for core in range(2):
            rows = fin[slot, pl.ds(core * 128, 128), :].astype(F32)
            res[core, :, cols] = (hid[core, :, cols] + gate[core][:, 0:1] * rows).astype(BF)
        leave.append(links.send(res.at[1 - c, :, cols], out.at[:, col], sib))
        keep = pltpu.make_async_copy(res.at[c, :, cols], out.at[:, col], local_sems.at[2 + slot])
        keep.start()
        stay.append(keep)
    for copy in leave:
        copy.wait_recv()
    for copy in stay:
        copy.wait()
    links.drain()


def scratch():
    def triple(shape):
        return [pltpu.VMEM(shape(STRIP), BF)] + [pltpu.VMEM(shape(3 * v), BF) for v in WIDTHS]

    return [
        pltpu.VMEM((2, 512, 2048), BF),
        pltpu.VMEM((2048, STRIP), BF),
        *[pltpu.VMEM((3, 2048, v), BF) for v in WIDTHS],
        pltpu.VMEM((2, 128, 4 * STRIP), BF),
        pltpu.VMEM((2, 128, 4 * STRIP), F32),
        *triple(lambda v: (4, 2, 128, v)),
        *triple(lambda v: (2, 128, v)),
        *triple(lambda v: (2, 2, 128, v)),
        pltpu.VMEM((2, 128, 128), F32),
        pltpu.VMEM((2, 128, 128), F32),
        pltpu.VMEM((4, 2, 8, 128), jnp.int32),
        pltpu.VMEM((2, 128, 128), F32),
        pltpu.VMEM((2, 4 * STRIP, 768), BF),
        pltpu.VMEM((1536, 1280), BF),
        pltpu.VMEM((4, 2, PAIR, 4 * STRIP), BF),
        pltpu.VMEM((4, 4, 2, PAIR, 4 * STRIP), BF),
        pltpu.VMEM((4, 4, PAIR, 1536), BF),
        pltpu.VMEM((4, 2, 4, PAIR, STRIP), BF),
        pltpu.VMEM((4, 2, 4, PAIR, STRIP), BF),
        pltpu.VMEM((4, 256, STRIP), BF),
        pltpu.VMEM((4, 256, STRIP), BF),
        pltpu.SemaphoreType.DMA((SENDS,)),
        pltpu.SemaphoreType.DMA((SENDS,)),
        pltpu.SemaphoreType.DMA((32,)),
    ]


ANY = pl.BlockSpec(memory_space=pl.ANY)
VM = pl.BlockSpec(memory_space=pltpu.VMEM)


def shards(attn, w_out, resid, norm_gain, route_ids, gate_vals, w_gate, w_up, w_down):
    core = lax.axis_index("expert") % 2
    ids = route_ids.reshape(-1)
    one_hot = (ids[:, None] == jnp.arange(8, dtype=jnp.int32)[None, :]).astype(jnp.int32)
    earlier = jnp.cumsum(one_hot, axis=0) - one_hot
    code = ids * PAIR + core * CAP + jnp.sum(earlier * one_hot, axis=1)
    return pl.pallas_call(
        layer,
        out_shape=jax.ShapeDtypeStruct(resid.shape, BF),
        in_specs=[ANY, ANY, ANY, VM, ANY, ANY, ANY, ANY, ANY],
        out_specs=ANY,
        scratch_shapes=scratch(),
        compiler_params=pltpu.CompilerParams(
            collective_id=0, has_side_effects=True, vmem_limit_bytes=62 * 2**20
        ),
        name="layer",
    )(
        attn,
        w_out,
        resid,
        norm_gain.reshape(1, -1),
        jnp.broadcast_to(code[None, :], (8, 128)),
        jnp.broadcast_to(gate_vals, (128, 128)),
        w_gate,
        w_up,
        w_down,
    )


def solution(mesh):
    placed = (
        P(("dp", "expert"), "tensor"),
        P("tensor", "expert"),
        P(("dp", "expert", "tensor"), None),
        P(),
        P(("dp", "expert", "tensor"), None),
        P(("dp", "expert", "tensor"), None),
        P("expert", None, "tensor"),
        P("expert", None, "tensor"),
        P("expert", "tensor", None),
    )
    return jax.shard_map(
        shards,
        mesh=mesh,
        in_specs=placed,
        out_specs=P(("dp", "expert", "tensor"), None),
        check_vma=False,
    )
```

```python
import functools

import jax
import jax.numpy as jnp
from jax import lax
from jax.experimental import pallas as pl
from jax.experimental.pallas import tpu as pltpu
from jax.sharding import PartitionSpec as P

MESH = pl.DeviceIdType.MESH
BF = jnp.bfloat16
F32 = jnp.float32

QN = 336
DN = 2048 - 4 * QN
QH = 176
PIECES = 5
WIDE = 128
STRIP = 640


class Place:
    def __init__(self):
        self.z = lax.axis_index("dp")
        self.e = lax.axis_index("expert")
        self.x = lax.axis_index("tensor")
        self.y = self.e // 2
        self.c = self.e % 2

    def at(self, dx=0, dy=0, dz=0, flip=False):
        core = 1 - self.c if flip else self.c
        return (
            lax.rem(self.z + dz, 4),
            lax.rem(self.y + dy, 4) * 2 + core,
            lax.rem(self.x + dx, 4),
        )


class Links:
    def __init__(self, send_sems, recv_sems):
        self.send_sems, self.recv_sems, self.open = send_sems, recv_sems, []

    def send(self, src, dst, device):
        i = len(self.open)
        copy = pltpu.make_async_remote_copy(
            src_ref=src,
            dst_ref=dst,
            send_sem=self.send_sems.at[i],
            recv_sem=self.recv_sems.at[i],
            device_id=device,
            device_id_type=MESH,
        )
        copy.start()
        self.open.append(copy)
        return copy

    def send_both(self, sources, dst, devices, core):
        i = len(self.open)
        copies = [
            pltpu.make_async_remote_copy(
                src_ref=sources[k],
                dst_ref=dst,
                send_sem=self.send_sems.at[i + k],
                recv_sem=self.recv_sems.at[i + core],
                device_id=devices[k],
                device_id_type=MESH,
            )
            for k in range(2)
        ]
        for copy in copies:
            copy.start()
        self.open.extend(copies)
        return [
            pltpu.make_async_remote_copy(
                src_ref=sources[k],
                dst_ref=dst,
                send_sem=self.send_sems.at[i + k],
                recv_sem=self.recv_sems.at[i + k],
                device_id=devices[k],
                device_id_type=MESH,
            )
            for k in range(2)
        ]

    def drain(self):
        for copy in self.open:
            copy.wait_send()


def greet(devices):
    barrier = pltpu.get_barrier_semaphore()
    for device in devices:
        pl.semaphore_signal(barrier, inc=1, device_id=device, device_id_type=MESH)
    pl.semaphore_wait(barrier, len(devices))


SENDS = 256
CAP = 24
PAIR = 2 * CAP
LAST = 3
PLAN = (
    "sq1", "siba", "sq0", "sd0", "wdx", "onq1", "onq0", "ownc", "sd1", "sq4", "sq3", "onz1", "owns",
    "rs1own", "onrq0", "ond0", "onrq1", "onz0", "onzo0", "onq4", "ond1", "sd4", "rs2own", "onzo1", "sq2",
    "across0", "onrq4", "onq3", "sides0", "rs10", "onz4", "sides1", "ond4", "across1", "sd3", "rs20",
    "onzo4", "onrq3", "onz3", "rs11", "code", "sd2", "sides4", "onq2", "across4", "rs14", "ond3", "onzo3",
    "sides3", "finown", "rs21", "onrq2", "rs24", "ond2", "across3", "fin0", "rs13", "onzo2", "onz2",
    "across2", "rs23", "sides2", "rs12", "fin1", "rs22", "fin4", "fin3", "fin2", "share", "codex", "norm",
    "disp0", "disp2", "spread0", "other", "disp3", "spread2", "disp1", "spread3", "wdz", "relay2", "spread1",
    "gu2", "act2", "relay1", "relay0", "ract2", "gu1", "act1", "wdw", "relay3", "down2", "gu0", "ract1",
    "act0", "gu3", "act3", "down1", "ract0", "down3", "down0", "homes", "comb2", "comb3", "comb1", "comb0",
    "out0", "out2", "out1", "out3",
)


def layer(
    attn, w_out, resid, gain, ids, gates, w_gate, w_up, w_down, out,
    a_buf, w_own, w, res, hid, hid_sib, p_own, parts, l_own, relays, f_own, finals,
    ssq, ssq_sib, code, w_gu, w_dn, sent, rows_in, act, done, back, comb, fin,
    send_sems, recv_sems, local_sems,
):
    me = Place()
    z, x, y, c = me.z, me.x, me.y, me.c
    sib = me.at(flip=True)
    xp, xm, xo = me.at(dx=1), me.at(dx=3), me.at(dx=2)
    yp, ym, zp, zm = me.at(dy=1), me.at(dy=3), me.at(dz=1), me.at(dz=3)
    links = Links(send_sems, recv_sems)

    load_w = [
        pltpu.make_async_copy(w_out.at[:, pl.ds(j * WIDE, WIDE)], w_own.at[j], local_sems.at[30 + j])
        for j in range(PIECES)
    ]
    for load in load_w:
        load.start()
    load_a = pltpu.make_async_copy(attn, a_buf.at[c], local_sems.at[1])
    load_a.start()
    load_r = []
    for b in range(4):
        col = pl.multiple_of((2 * b + c) * STRIP, 128)
        load = pltpu.make_async_copy(
            resid.at[:, pl.ds(col, STRIP)], res.at[c, :, pl.ds(b * STRIP, STRIP)], local_sems.at[2 + b]
        )
        load.start()
        load_r.append(load)

    loads = []
    for half in range(2):
        for b in range(4):
            source = pl.ds((2 * b + half) * STRIP, STRIP)
            target = pl.ds(b * STRIP, STRIP)
            for k, weight in enumerate((w_gate, w_up)):
                loads.append((weight.at[0, source], w_gu.at[half, target, pl.ds(k * 384, 384)]))
    quarter = pl.ds(pl.multiple_of(x * 1280, 128), 1280)
    loads.append((w_down.at[0, :, quarter], w_dn.at[pl.ds(0, 384)]))
    loads = [
        pltpu.make_async_copy(source, target, local_sems.at[7 + k])
        for k, (source, target) in enumerate(loads)
    ]

    def chip(dy, dx=0):
        return [(z, lax.rem(y + dy, 4) * 2 + core, lax.rem(x + dx, 4)) for core in range(2)]

    zo_, xs = me.at(dz=2), (None, xp, xo, xm)
    greet([sib, *chip(1), *chip(2), *chip(3), zp, zm, zo_, *chip(0, 1), *chip(0, 2), *chip(0, 3)])
    for load in loads:
        load.start()

    def rows_q(half=None):
        start = z * QN
        if half is None:
            return pl.ds(pl.multiple_of(start, 16), QN)
        return pl.ds(pl.multiple_of(start + half * QH, 16), QN - QH if half else QH)

    rows_d = pl.ds(4 * QN, DN)

    def rows_dh(half):
        return pl.ds(4 * QN + half * (DN // 2), DN // 2)

    def own(j, rows):
        return w_own.at[j, rows]

    def send_q(j):
        return (
            links.send(own(j, rows_q()), w.at[j, 1, rows_q()], yp),
            links.send(own(j, rows_q()), w.at[j, 0, rows_q()], ym),
        )

    def send_d(j):
        return (
            links.send(own(j, rows_d), w.at[j, 1, rows_d], yp),
            links.send(own(j, rows_d), w.at[j, 0, rows_d], ym),
        )

    n = PIECES
    q, d, rq, rd, zs, zo, zr, side, first, second = ({} for _ in range(10))
    steps = {}

    def step(name, run, *args):
        steps[name] = functools.partial(run, *args)

    loaded = set()

    def need(j):
        if j not in loaded:
            load_w[j].wait()
            loaded.add(j)

    def start_q(j):
        need(j)
        q[j] = send_q(j)

    def start_d(j):
        need(j)
        d[j] = send_d(j)

    def start_sibling():
        side["attn"] = links.send(attn, a_buf.at[c], sib)
        side["resid"] = []
        for b in range(4):
            col = pl.multiple_of((2 * b + 1 - c) * STRIP, 128)
            side["resid"].append(
                links.send(resid.at[:, pl.ds(col, STRIP)], res.at[c, :, pl.ds(b * STRIP, STRIP)], sib)
            )

    dn_rows = pl.multiple_of(z * 96, 16)
    dn_x, dn_z = {}, []

    def start_dn():
        for dx in (1, 3, 2):
            column = pl.multiple_of(lax.rem(x + dx, 4) * 1280, 128)
            dn_x[4 - dx] = links.send(
                w_down.at[0, pl.ds(dn_rows, 96), pl.ds(column, 1280)],
                w_dn.at[pl.ds((4 - dx) * 384 + dn_rows, 96)],
                xs[dx],
            )

    def share_dn():
        for slot in (3, 1, 2):
            dn_x[slot].wait_recv()
            piece = w_dn.at[pl.ds(slot * 384 + dn_rows, 96)]
            dn_z.extend(links.send(piece, piece, device) for device in (zp, zm, zo_))

    def wait_dn():
        for copy in dn_z:
            copy.wait_recv()

    def multiply(blocks, part, core, col):
        def step(m, carry):
            rows = pl.ds(pl.multiple_of(m * 256, 256), 256)
            right = blocks[0][...]
            if len(blocks) > 1:
                right = jnp.concatenate([block[...] for block in blocks], axis=1)
            result = jnp.dot(a_buf[core, rows, :], right, preferred_element_type=F32).astype(BF)
            cols = pl.ds(col, right.shape[1])
            part[2 * m, core, :, cols] = result[:128]
            part[2 * m + 1, core, :, cols] = result[128:]
            return carry

        lax.fori_loop(0, 2, step, 0)

    ahead, behind, over = lax.rem(x + 1, 4), lax.rem(x + 3, 4), lax.rem(x + 2, 4)

    def reduce_first(part, relay, final):
        return (
            links.send(part.at[over, 0], relay.at[0], xp),
            links.send(part.at[over, 1], relay.at[1], xm),
            links.send(part.at[ahead, 1], final.at[0, 1], xp),
            links.send(part.at[behind, 0], final.at[1, 0], xm),
        )

    def reduce_second(first, part, relay, final):
        first[0].wait_recv()
        part[ahead, 0] = (part[ahead, 0].astype(F32) + relay[0].astype(F32)).astype(BF)
        one = links.send(part.at[ahead, 0], final.at[0, 0], xp)
        first[1].wait_recv()
        part[behind, 1] = (part[behind, 1].astype(F32) + relay[1].astype(F32)).astype(BF)
        two = links.send(part.at[behind, 1], final.at[1, 1], xm)
        return (first[2], first[3], one, two)

    def on_q(j):
        q[j][0].wait_recv()
        one = links.send(w.at[j, 1, rows_q(0)], w.at[j, 2, rows_q(0)], yp)
        z_a = (
            links.send(w.at[j, 1, rows_q()], w.at[j, 1, rows_q()], zp),
            links.send(w.at[j, 1, rows_q()], w.at[j, 1, rows_q()], zm),
        )
        q[j][1].wait_recv()
        two = links.send(w.at[j, 0, rows_q(1)], w.at[j, 2, rows_q(1)], ym)
        z_b = (
            links.send(w.at[j, 0, rows_q()], w.at[j, 0, rows_q()], zp),
            links.send(w.at[j, 0, rows_q()], w.at[j, 0, rows_q()], zm),
        )
        rq[j] = (one, two)
        zs[j] = (z_a, z_b)

    def on_rq(j):
        rq[j][0].wait_recv()
        rq[j][1].wait_recv()
        zo[j] = (
            links.send(w.at[j, 2, rows_q()], w.at[j, 2, rows_q()], zp),
            links.send(w.at[j, 2, rows_q()], w.at[j, 2, rows_q()], zm),
        )

    def on_d(j):
        d[j][0].wait_recv()
        one = links.send(w.at[j, 1, rows_dh(0)], w.at[j, 2, rows_dh(0)], yp)
        d[j][1].wait_recv()
        two = links.send(w.at[j, 0, rows_dh(1)], w.at[j, 2, rows_dh(1)], ym)
        rd[j] = (one, two)

    def z_relay(j, pair, slot):
        low = pl.ds(pl.multiple_of(lax.rem(z + 3, 4) * QN, 16), QH)
        high = pl.ds(pl.multiple_of(lax.rem(z + 1, 4) * QN + QH, 16), QN - QH)
        pair[0].wait_recv()
        one = links.send(w.at[j, slot, low], w.at[j, slot, low], zp)
        pair[1].wait_recv()
        two = links.send(w.at[j, slot, high], w.at[j, slot, high], zm)
        zr[j, slot] = (one, two)

    def on_z(j):
        z_relay(j, zs[j][0], 1)
        z_relay(j, zs[j][1], 0)

    def on_zo(j):
        z_relay(j, zo[j], 2)

    def sides(j):
        for copy in (*zr[j, 0], *zr[j, 1]):
            copy.wait_recv()
        for core in range(2):
            multiply([w.at[j, 0], w.at[j, 1]], parts.at[j], core, 0)

    def across(j):
        for copy in (*rd[j], *zr[j, 2]):
            copy.wait_recv()
        for core in range(2):
            multiply([w.at[j, 2]], parts.at[j], core, 2 * WIDE)

    def group(j):
        return (p_own, l_own, f_own) if j == "own" else (parts.at[j], relays.at[j], finals.at[j])

    def first_half(j):
        first[j] = reduce_first(*group(j))

    def second_half(j):
        second[j] = reduce_second(first[j], *group(j))

    own_pieces = [w_own.at[j] for j in range(PIECES)]

    def own_tokens():
        load_a.wait()
        for j in range(n):
            need(j)
        multiply(own_pieces, p_own, c, 0)

    def sibling_tokens():
        side["attn"].wait_recv()
        multiply(own_pieces, p_own, 1 - c, 0)

    def place_tokens():
        experts = lax.broadcasted_iota(jnp.int32, (8, 128), 0)
        named = ids[...] == experts
        counts = named.astype(F32)
        before = lax.broadcasted_iota(jnp.int32, (128, 128), 0) < lax.broadcasted_iota(
            jnp.int32, (128, 128), 1
        )
        earlier = jnp.dot(counts.astype(BF), before.astype(F32).astype(BF), preferred_element_type=F32)
        slots = jnp.sum(jnp.where(named, earlier, 0.0), axis=0, keepdims=True).astype(jnp.int32)
        code[0, c] = jnp.broadcast_to(ids[...] * PAIR + c * CAP + slots, (8, 128))
        side["code"] = links.send(code.at[0, c], code.at[0, c], sib)

    def share_code():
        side["code"].wait_recv()
        side["codes"] = [links.send(code.at[0], code.at[4 - dx], xs[dx]) for dx in (1, 3, 2)]

    def finish(group, part, final, strips, width):
        for copy in second[group]:
            copy.wait_recv()
        for k, (col, strip) in enumerate(strips):
            cols = pl.ds(col, width)
            for core in range(2):
                at = pl.ds(k * width, width)
                total = (
                    res[core, :, cols].astype(F32)
                    + part[x, core, :, at].astype(F32)
                    + final[0, core, :, at].astype(F32)
                    + final[1, core, :, at].astype(F32)
                )
                hid[core, :, cols] = total
                add = jnp.sum(total * total, axis=1, keepdims=True)
                ssq[core] = ssq[core] + jnp.broadcast_to(add, (128, 128))

    ssq[...] = jnp.zeros_like(ssq)

    def finish_piece(j):
        strips = [
            (pl.multiple_of(lax.rem(y + dy, 4) * STRIP + j * WIDE, 128), k)
            for k, dy in enumerate((1, 3, 2))
        ]
        finish(j, parts.at[j], finals.at[j], strips, WIDE)

    def finish_own():
        for load in load_r:
            load.wait()
        for copy in side["resid"]:
            copy.wait_recv()
        finish("own", p_own, f_own, [(pl.multiple_of(y * STRIP, 128), 0)], STRIP)

    def start_share():
        side["ssq"] = links.send(ssq, ssq_sib, sib)

    def start_other():
        side["hid"] = links.send(hid.at[1 - c], hid_sib, sib)


    def pick(slot, chips):
        blocks = []
        for dy in chips:
            base = lax.rem(y + dy, 4) * (2 * PAIR)
            place = base + lax.broadcasted_iota(jnp.int32, (2 * PAIR, 128), 0)
            blocks.append(
                jnp.concatenate(
                    [
                        (place == code[slot, core, 0:1, :]).astype(F32).astype(BF)
                        for core in range(2)
                    ],
                    axis=1,
                )
            )
        return blocks[0] if len(blocks) == 1 else jnp.concatenate(blocks, axis=0)

    def normalize():
        side["ssq"].wait_recv()
        for core in range(2):
            scale = lax.rsqrt((ssq[core] + ssq_sib[core])[:, 0:1] / 5120.0 + 1e-06)
            for b in range(4):
                cols = pl.ds(b * STRIP, STRIP)
                col = pl.multiple_of((2 * b + c) * STRIP, 128)
                res[core, :, cols] = (hid[core, :, cols] * scale * gain[0:1, pl.ds(col, STRIP)]).astype(BF)
        for load in loads:
            load.wait()

    arrive = {}

    def dispatch(r):
        dy = (4 - r) % 4
        choice = pick(0, (dy,))
        for b in range(4):
            cols = pl.ds(b * STRIP, STRIP)
            normed = res[:, :, cols].reshape(256, STRIP)
            rows = jnp.dot(choice, normed, preferred_element_type=F32).astype(BF)
            sent[dy, :, :, cols] = rows.reshape(2, PAIR, STRIP)
        slot = (4 - dy) % 4
        if dy == 0:
            arrive[0] = [links.send(sent.at[0, 1 - c], rows_in.at[0, 0, c], sib)]
            rows_in[0, 0, c] = sent[0, c]
        else:
            arrive[slot] = links.send_both(
                [sent.at[dy, 0], sent.at[dy, 1]], rows_in.at[slot, 0, c], chip(dy), c
            )

    spread, relay_x = {}, {}

    def spread_rows(r):
        for copy in arrive[r]:
            copy.wait_recv()
        spread[r] = (
            links.send(rows_in.at[r, 0], rows_in.at[r, 3], xp),
            links.send(rows_in.at[r, 0], rows_in.at[r, 1], xm),
        )

    def relay_rows(r):
        spread[r][0].wait_recv()
        one = links.send(rows_in.at[r, 3, 0], rows_in.at[r, 2, 0], xp)
        spread[r][1].wait_recv()
        two = links.send(rows_in.at[r, 1, 1], rows_in.at[r, 2, 1], xm)
        relay_x[r] = (one, two)

    act_x = {}

    def gate_up(r):
        for copy in relay_x[r]:
            copy.wait_recv()
        both = jnp.dot(
            rows_in[r, :, 0].reshape(4 * PAIR, 4 * STRIP), w_gu[0], preferred_element_type=F32
        ) + jnp.dot(
            rows_in[r, :, 1].reshape(4 * PAIR, 4 * STRIP), w_gu[1], preferred_element_type=F32
        )
        left, right = both[:, :384], both[:, 384:]
        made = (left / (1.0 + jnp.exp(-left)) * right).astype(BF).reshape(4, PAIR, 384)
        for slot in range(4):
            act[r, lax.rem(x + slot, 4), :, pl.ds(0, 384)] = made[slot]

    def spread_act(r):
        mine = act.at[r, :, :, pl.ds(0, 384)]
        act_x[r] = [
            links.send(mine, act.at[r, :, :, pl.ds((4 - dx) * 384, 384)], xs[dx])
            for dx in ((2, 1, 3) if r == LAST else (1, 3))
        ]

    def relay_act(r):
        for k, (device, slot) in enumerate(((xp, 3), (xm, 1))):
            act_x[r][k].wait_recv()
            half = pl.ds(2 * k, 2)
            act_x[r].append(
                links.send(
                    act.at[r, half, :, pl.ds(slot * 384, 384)], act.at[r, half, :, pl.ds(768, 384)], device
                )
            )

    home = {}

    def down(r):
        final = r == LAST
        for copy in act_x[r][-3 if final else -2:]:
            copy.wait_recv()
        whole = jnp.dot(
            act[r].reshape(4 * PAIR, 1536), w_dn[...], preferred_element_type=F32
        ).astype(BF).reshape(4, PAIR, 1280)
        for core in range(2):
            done[r, core] = whole[:, :, core * STRIP:(core + 1) * STRIP]
        slot = (4 - r) % 4
        if r == 0:
            home[0] = [links.send(done.at[0, 1 - c], back.at[0, c], sib)]
            back[0, c] = done[0, c]
        elif not final:
            home[slot] = links.send_both([done.at[r, 0], done.at[r, 1]], back.at[slot, c], chip(r), c)
        else:
            home[slot] = []
            for dx in (2, 1, 3, 0):
                t = lax.rem(x + dx, 4)
                home[slot].append(
                    links.send_both(
                        [done.at[r, 0, t], done.at[r, 1, t]], back.at[slot, c, t], chip(r), c
                    )
                )

    ending = (4 - LAST) % 4

    def wait_home():
        for copy in side["codes"]:
            copy.wait_recv()
        for slot in range(4):
            if slot != ending:
                for copy in home[slot]:
                    copy.wait_recv()

    over_x = {}

    def combine(dx):
        for copy in home[ending][(2, 1, 3, 0).index(dx)]:
            copy.wait_recv()
        t = lax.rem(x + dx, 4)
        mixed = lax.dot_general(
            pick(dx, (0, 1, 2, 3)),
            back[:, :, t].reshape(8 * PAIR, STRIP),
            (((0,), (0,)), ((), ())),
            preferred_element_type=F32,
        ).astype(BF)
        comb[dx] = mixed.reshape(2, 128, STRIP)
        if dx:
            over_x[4 - dx] = links.send_both(
                [comb.at[dx, 0], comb.at[dx, 1]], fin.at[4 - dx, c], chip(0, dx), c
            )
        else:
            over_x[0] = [links.send(comb.at[0, 1 - c], fin.at[0, c], sib)]
            fin[0, c] = comb[0, c]

    square = lax.broadcasted_iota(jnp.int32, (128, 128), 0) == lax.broadcasted_iota(
        jnp.int32, (128, 128), 1
    )
    weight = jnp.sum(jnp.where(square, gates[...], 0.0), axis=1, keepdims=True)
    stay = []

    def output(slot):
        if not stay:
            side["hid"].wait_recv()
        for copy in over_x[slot]:
            copy.wait_recv()
        b = lax.rem(x + slot, 4)
        cols = pl.ds(pl.multiple_of(b * STRIP, 128), STRIP)
        for half, rows in enumerate((hid.at[c], hid_sib)):
            core = c if half == 0 else 1 - c
            total = rows[:, cols] + weight * fin[slot, core].astype(F32)
            res[core, :, cols] = total.astype(BF)
            col = pl.ds(pl.multiple_of((2 * b + core) * STRIP, 128), STRIP)
            keep = pltpu.make_async_copy(
                res.at[core, :, cols], out.at[:, col], local_sems.at[2 * slot + half]
            )
            keep.start()
            stay.append(keep)

    step("siba", start_sibling)
    step("wdx", start_dn)
    step("wdz", share_dn)
    step("wdw", wait_dn)
    step("ownc", own_tokens)
    step("owns", sibling_tokens)
    step("code", place_tokens)
    step("codex", share_code)
    step("rs1own", first_half, "own")
    step("rs2own", second_half, "own")
    step("finown", finish_own)
    for j in range(n):
        step(f"sq{j}", start_q, j)
        step(f"sd{j}", start_d, j)
        step(f"onq{j}", on_q, j)
        step(f"onrq{j}", on_rq, j)
        step(f"ond{j}", on_d, j)
        step(f"onz{j}", on_z, j)
        step(f"onzo{j}", on_zo, j)
        step(f"sides{j}", sides, j)
        step(f"across{j}", across, j)
        step(f"rs1{j}", first_half, j)
        step(f"rs2{j}", second_half, j)
        step(f"fin{j}", finish_piece, j)
    step("share", start_share)
    step("other", start_other)
    step("norm", normalize)
    for r in range(4):
        step(f"disp{r}", dispatch, r)
        step(f"spread{r}", spread_rows, r)
        step(f"relay{r}", relay_rows, r)
        step(f"gu{r}", gate_up, r)
        step(f"act{r}", spread_act, r)
        step(f"ract{r}", relay_act, r)
        step(f"down{r}", down, r)
        step(f"comb{r}", combine, r)
        step(f"out{r}", output, r)
    step("homes", wait_home)
    for name in PLAN:
        steps.pop(name)()
    steps.pop(f"ract{LAST}")
    assert not steps
    for copy in stay:
        copy.wait()
    links.drain()


def scratch():
    wide = 3 * WIDE
    return [
        pltpu.VMEM((2, 512, 2048), BF),
        pltpu.VMEM((PIECES, 2048, WIDE), BF),
        pltpu.VMEM((PIECES, 3, 2048, WIDE), BF),
        pltpu.VMEM((2, 128, 4 * STRIP), BF),
        pltpu.VMEM((2, 128, 4 * STRIP), F32),
        pltpu.VMEM((128, 4 * STRIP), F32),
        pltpu.VMEM((4, 2, 128, STRIP), BF),
        pltpu.VMEM((PIECES, 4, 2, 128, wide), BF),
        pltpu.VMEM((2, 128, STRIP), BF),
        pltpu.VMEM((PIECES, 2, 128, wide), BF),
        pltpu.VMEM((2, 2, 128, STRIP), BF),
        pltpu.VMEM((PIECES, 2, 2, 128, wide), BF),
        pltpu.VMEM((2, 128, 128), F32),
        pltpu.VMEM((2, 128, 128), F32),
        pltpu.VMEM((4, 2, 8, 128), jnp.int32),
        pltpu.VMEM((2, 4 * STRIP, 768), BF),
        pltpu.VMEM((1536, 1280), BF),
        pltpu.VMEM((4, 2, PAIR, 4 * STRIP), BF),
        pltpu.VMEM((4, 4, 2, PAIR, 4 * STRIP), BF),
        pltpu.VMEM((4, 4, PAIR, 1536), BF),
        pltpu.VMEM((4, 2, 4, PAIR, STRIP), BF),
        pltpu.VMEM((4, 2, 4, PAIR, STRIP), BF),
        pltpu.VMEM((4, 2, 128, STRIP), BF),
        pltpu.VMEM((4, 2, 128, STRIP), BF),
        pltpu.SemaphoreType.DMA((SENDS,)),
        pltpu.SemaphoreType.DMA((SENDS,)),
        pltpu.SemaphoreType.DMA((40,)),
    ]


ANY = pl.BlockSpec(memory_space=pl.ANY)
VM = pl.BlockSpec(memory_space=pltpu.VMEM)


def shards(attn, w_out, resid, norm_gain, route_ids, gate_vals, w_gate, w_up, w_down):
    return pl.pallas_call(
        layer,
        out_shape=jax.ShapeDtypeStruct(resid.shape, BF),
        in_specs=[ANY, ANY, ANY, VM, VM, VM, ANY, ANY, ANY],
        out_specs=ANY,
        scratch_shapes=scratch(),
        compiler_params=pltpu.CompilerParams(
            collective_id=0, has_side_effects=True, vmem_limit_bytes=62 * 2**20
        ),
        name="layer",
    )(
        attn,
        w_out,
        resid,
        norm_gain.reshape(1, -1),
        route_ids.reshape(1, -1),
        gate_vals.reshape(1, -1),
        w_gate,
        w_up,
        w_down,
    )


def solution(mesh):
    placed = (
        P(("dp", "expert"), "tensor"),
        P("tensor", "expert"),
        P(("dp", "expert", "tensor"), None),
        P(),
        P(("dp", "expert", "tensor"), None),
        P(("dp", "expert", "tensor"), None),
        P("expert", None, "tensor"),
        P("expert", None, "tensor"),
        P("expert", "tensor", None),
    )
    return jax.shard_map(
        shards,
        mesh=mesh,
        in_specs=placed,
        out_specs=P(("dp", "expert", "tensor"), None),
        check_vma=False,
    )
```

```python
import functools

import jax
import jax.numpy as jnp
from jax import lax
from jax.experimental import pallas as pl
from jax.experimental.pallas import tpu as pltpu
from jax.sharding import PartitionSpec as P

MESH = pl.DeviceIdType.MESH
BF = jnp.bfloat16
F32 = jnp.float32

QN = 336
DN = 2048 - 4 * QN
QH = 176
PIECES = 5
WIDE = 128
STRIP = 640
FRONT = 2 * STRIP


class Place:
    def __init__(self):
        self.z = lax.axis_index("dp")
        self.e = lax.axis_index("expert")
        self.x = lax.axis_index("tensor")
        self.y = self.e // 2
        self.c = self.e % 2

    def at(self, dx=0, dy=0, dz=0, flip=False):
        core = 1 - self.c if flip else self.c
        return (
            lax.rem(self.z + dz, 4),
            lax.rem(self.y + dy, 4) * 2 + core,
            lax.rem(self.x + dx, 4),
        )


class Links:
    def __init__(self, send_sems, recv_sems):
        self.send_sems, self.recv_sems = send_sems, recv_sems
        self.free, self.made, self.landings, self.open = [], 0, 0, []

    def landing(self):
        self.landings += 1
        return self.landings - 1

    def send(self, src, dst, device, landing=None):
        if not self.free:
            self.free.append(self.made)
            self.made += 1
        i = self.free.pop(0)
        copy = pltpu.make_async_remote_copy(
            src_ref=src,
            dst_ref=dst,
            send_sem=self.send_sems.at[i],
            recv_sem=self.recv_sems.at[self.landing() if landing is None else landing],
            device_id=device,
            device_id_type=MESH,
        )
        copy.start()
        self.open.append((copy, i))
        return copy

    def send_both(self, sources, dst, devices, landing):
        for source, device in zip(sources, devices):
            self.send(source, dst, device, landing)

    def landed(self, landing, dst, device):
        pltpu.make_async_remote_copy(
            src_ref=dst,
            dst_ref=dst,
            send_sem=self.send_sems.at[0],
            recv_sem=self.recv_sems.at[landing],
            device_id=device,
            device_id_type=MESH,
        ).wait_recv()

    def settle(self, count):
        done, self.open = self.open[:count], self.open[count:]
        for copy, i in done:
            copy.wait_send()
            self.free.append(i)

    def settle_through(self, last):
        for k, (copy, _) in enumerate(self.open):
            if copy is last:
                self.settle(k + 1)
                return

    def settle_all_but(self, count):
        self.settle(max(0, len(self.open) - count))


def greet(devices):
    for device in devices:
        pl.semaphore_signal(
            pltpu.get_barrier_semaphore(), inc=1, device_id=device, device_id_type=MESH
        )


SENDS = 92
LANDINGS = 167
KEEP = 48
CAP = 24
PAIR = 2 * CAP
LAST = 3
OWN = PIECES
(
    TO_SIBLING, DOWN_X, DOWN_Z, DOWN_WAIT, OWN_TOKENS, SIBLING_TOKENS, PLACE, PLACE_X, PLACE_WAIT, SUM_SEND,
    SUM_AHEAD, SUM_BEHIND, SUM_END, SEND_Q, SEND_D, Q_BEHIND, Q_AHEAD, Q_ACROSS, D_HERE, Z_BEHIND, Z_AHEAD,
    Z_ACROSS, MUL_SIDES, MUL_ACROSS, SQUARES, HIDDEN, NORM, ROWS_Y, ROWS_X, ROWS_AHEAD, ROWS_BEHIND, SHOW,
    SHOW_AHEAD, SHOW_BEHIND, SHOW_WAIT, SHOWN_Y, SHOWN_WAIT, GATE_UP, ACT_X, ACT_RELAY, DOWN, HOME, COMBINE,
    OUT,
) = range(44)
PLAN = (
    (SEND_Q, 0), (TO_SIBLING,), (OWN_TOKENS,), (SEND_Q, 2), (Q_BEHIND, 0), (Q_AHEAD, 0), (DOWN_X,),
    (SEND_Q, 1), (SEND_D, 2), (Q_BEHIND, 2), (Q_AHEAD, 2), (PLACE,), (Z_AHEAD, 0), (SEND_D, 0),
    (Q_BEHIND, 1), (SEND_D, 1), (SIBLING_TOKENS,), (Q_ACROSS, 2), (Q_AHEAD, 1), (SUM_SEND, OWN),
    (Z_BEHIND, 2), (D_HERE, 2), (Z_AHEAD, 2), (Q_ACROSS, 0), (Z_ACROSS, 2), (Z_BEHIND, 1), (SEND_Q, 4),
    (SUM_AHEAD, OWN), (PLACE_X,), (SUM_BEHIND, OWN), (Z_BEHIND, 0), (D_HERE, 0), (Q_ACROSS, 1),
    (MUL_SIDES, 2), (Z_ACROSS, 0), (D_HERE, 1), (MUL_ACROSS, 2), (SUM_SEND, 2), (Q_BEHIND, 4), (Q_AHEAD, 4),
    (SEND_Q, 3), (MUL_SIDES, 0), (Z_AHEAD, 1), (SEND_D, 4), (MUL_ACROSS, 0), (SUM_END, OWN), (SUM_SEND, 0),
    (Z_ACROSS, 1), (Q_ACROSS, 4), (Z_BEHIND, 4), (Z_AHEAD, 4), (SUM_AHEAD, 2), (Q_BEHIND, 3), (Q_AHEAD, 3),
    (SEND_D, 3), (SUM_BEHIND, 2), (PLACE_WAIT,), (MUL_SIDES, 1), (MUL_ACROSS, 1), (SUM_SEND, 1), (D_HERE, 4),
    (Z_ACROSS, 4), (Q_ACROSS, 3), (MUL_SIDES, 4), (Z_BEHIND, 3), (SUM_BEHIND, 0), (SUM_AHEAD, 0),
    (D_HERE, 3), (Z_AHEAD, 3), (SUM_AHEAD, 1), (SUM_BEHIND, 1), (MUL_ACROSS, 4), (Z_ACROSS, 3),
    (SUM_SEND, 4), (MUL_SIDES, 3), (MUL_ACROSS, 3), (SUM_SEND, 3), (SUM_BEHIND, 4), (DOWN_Z,), (SUM_END, 0),
    (SUM_END, 2), (SUM_AHEAD, 4), (SUM_AHEAD, 3), (SUM_BEHIND, 3), (SUM_END, 1), (SUM_END, 4), (SUM_END, 3),
    (SQUARES,), (NORM,), (ROWS_Y, 2), (SHOW,), (ROWS_Y, 0), (SHOWN_Y, 0, 0), (SHOWN_Y, 1, 0), (ROWS_X, 2),
    (SHOWN_Y, 2, 0), (ROWS_Y, 3), (ROWS_Y, 1), (SHOW_BEHIND,), (SHOW_AHEAD,), (SHOWN_Y, 2, 1),
    (ROWS_BEHIND, 2), (ROWS_X, 1), (SHOWN_Y, 2, 3), (ROWS_AHEAD, 2), (SHOW_WAIT,), (ROWS_X, 0),
    (SHOWN_Y, 2, 2), (ROWS_AHEAD, 1), (SHOWN_Y, 1, 2), (SHOWN_Y, 1, 1), (SHOWN_Y, 0, 1), (SHOWN_Y, 1, 3),
    (SHOWN_Y, 0, 3), (SHOWN_Y, 3, 1), (ROWS_BEHIND, 1), (SHOWN_Y, 3, 0), (SHOWN_WAIT, 2), (GATE_UP, 2),
    (ACT_X, 2), (SHOWN_Y, 0, 2), (SHOWN_Y, 3, 3), (ROWS_X, 3), (ACT_RELAY, 2), (ROWS_BEHIND, 0),
    (ROWS_AHEAD, 0), (SHOWN_Y, 3, 2), (ROWS_BEHIND, 3), (ROWS_AHEAD, 3), (SHOWN_WAIT, 1), (SHOWN_WAIT, 0),
    (DOWN_WAIT,), (GATE_UP, 1), (ACT_X, 1), (DOWN, 2), (GATE_UP, 0), (ACT_X, 0), (SHOWN_WAIT, 3),
    (GATE_UP, 3), (ACT_RELAY, 1), (ACT_X, 3), (DOWN, 1), (HIDDEN,), (ACT_RELAY, 0), (DOWN, 3), (DOWN, 0),
    (HOME,), (COMBINE, 2), (COMBINE, 1), (COMBINE, 0), (COMBINE, 3), (OUT, 2), (OUT, 0), (OUT, 3), (OUT, 1),
)


def layer(
    attn, w_out, resid, gain, ids, gates, w_gate, w_up, w_down, out,
    a_buf, w_own, w, res, hid, hid_sib, p_own, parts, l_own, relays, f_own, finals,
    ssq, ssq_sib, code, w_gu, w_dn, rows_in, near, sown, act, done, back, fin,
    send_sems, recv_sems, local_sems,
):
    me = Place()
    z, x, y, c = me.z, me.x, me.y, me.c
    sib = me.at(flip=True)
    xp, xm, xo = me.at(dx=1), me.at(dx=3), me.at(dx=2)
    yp, ym, zp, zm = me.at(dy=1), me.at(dy=3), me.at(dz=1), me.at(dz=3)
    links = Links(send_sems, recv_sems)

    def chip(dy, dx=0):
        return [(z, lax.rem(y + dy, 4) * 2 + core, lax.rem(x + dx, 4)) for core in range(2)]

    zo_, xs = me.at(dz=2), (None, xp, xo, xm)
    friends = [sib, *chip(1), *chip(2), *chip(3), zp, zm, zo_, *chip(0, 1), *chip(0, 2), *chip(0, 3)]
    greet(friends)

    load_w = [
        pltpu.make_async_copy(w_out.at[:, pl.ds(j * WIDE, WIDE)], w_own.at[j], local_sems.at[j])
        for j in range(PIECES)
    ]
    for load in load_w:
        load.start()
    load_a = pltpu.make_async_copy(attn, a_buf.at[c], local_sems.at[5])
    load_a.start()
    for b in range(4):
        col = pl.multiple_of((2 * b + c) * STRIP, 128)
        load = pltpu.make_async_copy(
            resid.at[:, pl.ds(col, STRIP)], res.at[c, :, pl.ds(b * STRIP, STRIP)], local_sems.at[6]
        )
        load.start()

    loads = []
    for half in range(2):
        for b in range(4):
            source = pl.ds((2 * b + half) * STRIP, STRIP)
            target = pl.ds(b * STRIP, STRIP)
            for k, weight in enumerate((w_gate, w_up)):
                loads.append((weight.at[0, source], w_gu.at[half, target, pl.ds(k * 384, 384)]))
    quarter = pl.ds(pl.multiple_of(x * 1280, 128), 1280)
    loads.append((w_down.at[0, :, quarter], w_dn.at[pl.ds(0, 384)]))
    loads = [
        pltpu.make_async_copy(source, target, local_sems.at[7 if k < 16 else 8])
        for k, (source, target) in enumerate(loads)
    ]

    pl.semaphore_wait(pltpu.get_barrier_semaphore(), len(friends))
    for load in loads:
        load.start()

    def rows_q(half=None):
        start = z * QN
        if half is None:
            return pl.ds(pl.multiple_of(start, 16), QN)
        return pl.ds(pl.multiple_of(start + half * QH, 16), QN - QH if half else QH)

    rows_d = pl.ds(4 * QN, DN)

    def rows_dh(half):
        return pl.ds(4 * QN + half * (DN // 2), DN // 2)

    def own(j, rows):
        return w_own.at[j, rows]

    def send_q(j):
        return (
            links.send(own(j, rows_q()), w.at[j, 1, rows_q()], yp),
            links.send(own(j, rows_q()), w.at[j, 0, rows_q()], ym),
        )

    def send_d(j):
        return (
            links.send(own(j, rows_d), w.at[j, 1, rows_d], yp),
            links.send(own(j, rows_d), w.at[j, 0, rows_d], ym),
        )

    n = PIECES
    q, d, zs, zo, side, first, front, lands = ({} for _ in range(8))
    rows_far = pl.ds(pl.multiple_of(lax.rem(z + 2, 4) * QN, 16), QN)

    def land(*key):
        if key not in lands:
            lands[key] = links.landing()
        return lands[key]

    steps = {}

    def step(kind, run, *args, given=None):
        steps[(kind, *(args if given is None else given))] = functools.partial(run, *args)

    loaded = set()

    def need(j):
        if j not in loaded:
            load_w[j].wait()
            loaded.add(j)

    def start_q(j):
        need(j)
        q[j] = send_q(j)

    def start_d(j):
        need(j)
        d[j] = send_d(j)

    def start_sibling():
        side["attn"] = links.send(attn, a_buf.at[c], sib)
        side["resid"] = links.landing()
        for b in range(4):
            col = pl.multiple_of((2 * b + 1 - c) * STRIP, 128)
            links.send(
                resid.at[:, pl.ds(col, STRIP)], res.at[c, :, pl.ds(b * STRIP, STRIP)], sib, side["resid"]
            )

    dn_rows = pl.multiple_of(z * 96, 16)
    dn_x, dn_z = {}, []

    def start_dn():
        for dx in (1, 3, 2):
            column = pl.multiple_of(lax.rem(x + dx, 4) * 1280, 128)
            dn_x[4 - dx] = links.send(
                w_down.at[0, pl.ds(dn_rows, 96), pl.ds(column, 1280)],
                w_dn.at[pl.ds((4 - dx) * 384 + dn_rows, 96)],
                xs[dx],
            )

    def share_dn():
        for slot in (3, 1, 2):
            dn_x[slot].wait_recv()
            piece = w_dn.at[pl.ds(slot * 384 + dn_rows, 96)]
            dn_z.extend(links.send(piece, piece, device) for device in (zp, zm, zo_))

    def wait_dn():
        for copy in dn_z:
            copy.wait_recv()

    def multiply(blocks, part, core, col):
        def step(m, carry):
            rows = pl.ds(pl.multiple_of(m * 256, 256), 256)
            right = blocks[0][...]
            if len(blocks) > 1:
                right = jnp.concatenate([block[...] for block in blocks], axis=1)
            result = jnp.dot(a_buf[core, rows, :], right, preferred_element_type=F32).astype(BF)
            cols = pl.ds(col, right.shape[1])
            part[2 * m, core, :, cols] = result[:128]
            part[2 * m + 1, core, :, cols] = result[128:]
            return carry

        lax.fori_loop(0, 2, step, 0)

    ahead, behind, over = lax.rem(x + 1, 4), lax.rem(x + 3, 4), lax.rem(x + 2, 4)

    def group(j):
        return (p_own, l_own, f_own) if j == OWN else (parts.at[j], relays.at[j], finals.at[j])

    def reduce_first(j):
        part, relay, final = group(j)
        first[j] = (
            links.send(part.at[over, 0], relay.at[0], xp),
            links.send(part.at[over, 1], relay.at[1], xm),
        )
        links.send(part.at[ahead, 1], final.at[0, 1], xp, land(j, "sum"))
        links.send(part.at[behind, 0], final.at[1, 0], xm, land(j, "sum"))

    def reduce_ahead(j):
        part, relay, final = group(j)
        first[j][0].wait_recv()
        part[ahead, 0] = (part[ahead, 0].astype(F32) + relay[0].astype(F32)).astype(BF)
        front[j, 0] = links.send(part.at[ahead, 0], final.at[0, 0], xp, land(j, "sum"))

    def reduce_behind(j):
        part, relay, final = group(j)
        first[j][1].wait_recv()
        part[behind, 1] = (part[behind, 1].astype(F32) + relay[1].astype(F32)).astype(BF)
        front[j, 1] = links.send(part.at[behind, 1], final.at[1, 1], xm, land(j, "sum"))

    def on_q_behind(j):
        q[j][0].wait_recv()
        links.send(w.at[j, 1, rows_q(0)], w.at[j, 2, rows_q(0)], yp, land(j, "rq"))
        zs[j, 1] = (
            links.send(w.at[j, 1, rows_q()], w.at[j, 1, rows_q()], zp),
            links.send(w.at[j, 1, rows_q()], w.at[j, 1, rows_q()], zm),
        )

    def on_q_ahead(j):
        q[j][1].wait_recv()
        links.send(w.at[j, 0, rows_q(1)], w.at[j, 2, rows_q(1)], ym, land(j, "rq"))
        zs[j, 0] = (
            links.send(w.at[j, 0, rows_q()], w.at[j, 0, rows_q()], zp),
            links.send(w.at[j, 0, rows_q()], w.at[j, 0, rows_q()], zm),
        )

    def on_rq(j):
        links.landed(land(j, "rq"), w.at[j, 2, rows_q()], yp)
        zo[j] = (
            links.send(w.at[j, 2, rows_q()], w.at[j, 2, rows_q()], zp),
            links.send(w.at[j, 2, rows_q()], w.at[j, 2, rows_q()], zm),
        )

    def on_d(j):
        d[j][0].wait_recv()
        links.send(w.at[j, 1, rows_dh(0)], w.at[j, 2, rows_dh(0)], yp, land(j, "rd"))
        d[j][1].wait_recv()
        links.send(w.at[j, 0, rows_dh(1)], w.at[j, 2, rows_dh(1)], ym, land(j, "rd"))

    def z_relay(j, pair, slot):
        low = pl.ds(pl.multiple_of(lax.rem(z + 3, 4) * QN, 16), QH)
        high = pl.ds(pl.multiple_of(lax.rem(z + 1, 4) * QN + QH, 16), QN - QH)
        pair[0].wait_recv()
        links.send(w.at[j, slot, low], w.at[j, slot, low], zp, land(j, slot))
        pair[1].wait_recv()
        links.send(w.at[j, slot, high], w.at[j, slot, high], zm, land(j, slot))

    def on_z(j, slot):
        z_relay(j, zs[j, slot], slot)

    def on_zo(j):
        z_relay(j, zo[j], 2)

    def sides(j):
        links.landed(land(j, 0), w.at[j, 0, rows_far], zp)
        links.landed(land(j, 1), w.at[j, 1, rows_far], zp)
        for core in range(2):
            multiply([w.at[j, 0], w.at[j, 1]], parts.at[j], core, 0)

    def across(j):
        links.landed(land(j, "rd"), w.at[j, 2, rows_d], yp)
        links.landed(land(j, 2), w.at[j, 2, rows_far], zp)
        links.settle_all_but(KEEP)
        for core in range(2):
            multiply([w.at[j, 2]], parts.at[j], core, 2 * WIDE)

    own_pieces = [w_own.at[j] for j in range(PIECES)]

    def own_tokens():
        load_a.wait()
        for j in range(n):
            need(j)
        multiply(own_pieces, p_own, c, 0)

    def sibling_tokens():
        side["attn"].wait_recv()
        multiply(own_pieces, p_own, 1 - c, 0)

    def place_tokens():
        experts = lax.broadcasted_iota(jnp.int32, (8, 128), 0)
        named = ids[...] == experts
        counts = named.astype(F32)
        before = lax.broadcasted_iota(jnp.int32, (128, 128), 0) < lax.broadcasted_iota(
            jnp.int32, (128, 128), 1
        )
        earlier = jnp.dot(counts.astype(BF), before.astype(F32).astype(BF), preferred_element_type=F32)
        slots = jnp.sum(jnp.where(named, earlier, 0.0), axis=0, keepdims=True).astype(jnp.int32)
        code[0, c] = jnp.broadcast_to(ids[...] * PAIR + c * CAP + slots, (8, 128))
        side["code"] = links.send(code.at[0, c], code.at[0, c], sib)

    def share_code():
        side["code"].wait_recv()
        side["codes"] = [links.send(code.at[0], code.at[4 - dx], xs[dx]) for dx in (1, 3, 2)]

    def finish(j, strips, width):
        part, _, final = group(j)
        links.landed(land(j, "sum"), final, xp)
        for k, (col, strip) in enumerate(strips):
            cols = pl.ds(col, width)
            for core in range(2):
                at = pl.ds(k * width, width)
                total = (
                    res[core, :, cols].astype(F32)
                    + part[x, core, :, at].astype(F32)
                    + final[0, core, :, at].astype(F32)
                    + final[1, core, :, at].astype(F32)
                )
                hid[core, :, cols] = total
                add = jnp.sum(total * total, axis=1, keepdims=True)
                ssq[core] = ssq[core] + jnp.broadcast_to(add, (128, 128))

    ssq[...] = jnp.zeros_like(ssq)

    def finish_piece(j):
        strips = [
            (pl.multiple_of(lax.rem(y + dy, 4) * STRIP + j * WIDE, 128), k)
            for k, dy in enumerate((1, 3, 2))
        ]
        finish(j, strips, WIDE)

    def finish_own(_):
        pltpu.make_async_copy(res.at[c], res.at[c], local_sems.at[6]).wait()
        links.landed(side["resid"], res.at[1 - c], sib)
        finish(OWN, [(pl.multiple_of(y * STRIP, 128), 0)], STRIP)

    def start_share():
        side["ssq"] = links.send(ssq, ssq_sib, sib)

    def start_other():
        side["hid"] = links.send(hid.at[1 - c], hid_sib, sib)


    def pick(slot, chips):
        blocks = []
        for dy in chips:
            base = lax.rem(y + dy, 4) * (2 * PAIR)
            place = base + lax.broadcasted_iota(jnp.int32, (2 * PAIR, 128), 0)
            blocks.append(
                jnp.concatenate(
                    [
                        (place == code[slot, core, 0:1, :]).astype(F32).astype(BF)
                        for core in range(2)
                    ],
                    axis=1,
                )
            )
        return blocks[0] if len(blocks) == 1 else jnp.concatenate(blocks, axis=0)

    def normalize():
        side["ssq"].wait_recv()
        for core in range(2):
            scale = lax.rsqrt((ssq[core] + ssq_sib[core])[:, 0:1] / 5120.0 + 1e-06)
            for b in range(4):
                cols = pl.ds(b * STRIP, STRIP)
                col = pl.multiple_of((2 * b + c) * STRIP, 128)
                res[core, :, cols] = (hid[core, :, cols] * scale * gain[0:1, pl.ds(col, STRIP)]).astype(BF)
        pltpu.make_async_copy(w_gu, w_gu, local_sems.at[7]).wait()
        loads[16].wait()
        links.settle_all_but(KEEP)

    arrive, come, shown = {}, {}, []
    early, later = pl.ds(0, FRONT), pl.ds(FRONT, FRONT)

    def sent(dy, core):
        return a_buf.at[0, pl.ds(pl.multiple_of((2 * dy + core) * PAIR, 16), PAIR), early]

    def dispatch(r):
        dy = (4 - r) % 4
        choice = pick(0, (dy,))
        normed = res[:, :, later].reshape(256, FRONT)
        rows = jnp.dot(choice, normed, preferred_element_type=F32).astype(BF)
        a_buf[0, pl.ds(2 * dy * PAIR, 2 * PAIR), early] = rows
        slot = (4 - dy) % 4
        if dy == 0:
            arrive[0] = links.send(sent(0, 1 - c), rows_in.at[0, 0, c, :, later], sib)
            rows_in[0, 0, c, :, later] = sent(0, c)[...]
        else:
            target = rows_in.at[slot, 0, c, :, later]
            links.send_both([sent(dy, 0), sent(dy, 1)], target, chip(dy), land("rows", slot))

    spread, relay_x = {}, {}

    def show_rows():
        shown.append(links.send(res.at[:, :, early], near.at[2], xp))
        shown.append(links.send(res.at[:, :, early], near.at[0], xm))
        front["shown"] = shown[-1]

    def show_on_ahead():
        shown[0].wait_recv()
        come[0] = links.send(near.at[2, 0], near.at[1, 0], xp)

    def show_on_behind():
        shown[1].wait_recv()
        come[1] = links.send(near.at[0, 1], near.at[1, 1], xm)

    def wait_shown():
        come[0].wait_recv()
        come[1].wait_recv()

    def dispatch_shown(r, t):
        dy = (4 - r) % 4
        source = res[:, :, early] if t == 0 else near[t - 1]
        rows = jnp.dot(pick(t, (dy,)), source.reshape(256, FRONT), preferred_element_type=F32)
        sown[r, t] = rows.astype(BF).reshape(2, PAIR, FRONT)
        target = rows_in.at[r, t, c, :, early]
        if r == 0:
            links.send(sown.at[r, t, 1 - c], target, sib, land("shown", r))
            rows_in[r, t, c, :, early] = sown[r, t, c]
        else:
            links.send_both([sown.at[r, t, 0], sown.at[r, t, 1]], target, chip(dy), land("shown", r))

    def wait_dispatched(r):
        links.settle_all_but(KEEP)
        whole = rows_in.at[0, :, 1 - c, :, early] if r == 0 else rows_in.at[r, :, :, :, early]
        links.landed(land("shown", r), whole, sib)

    spread, relay_x = {}, {}

    def spread_rows(r):
        if r == 0:
            arrive[0].wait_recv()
        else:
            links.landed(land("rows", r), rows_in.at[r, 0, :, :, later], sib)
        mine = rows_in.at[r, 0, :, :, later]
        spread[r] = (
            links.send(mine, rows_in.at[r, 3, :, :, later], xp),
            links.send(mine, rows_in.at[r, 1, :, :, later], xm),
        )

    def relay_ahead(r):
        spread[r][0].wait_recv()
        relay_x[r, 0] = links.send(rows_in.at[r, 3, 0, :, later], rows_in.at[r, 2, 0, :, later], xp)

    def relay_behind(r):
        spread[r][1].wait_recv()
        relay_x[r, 1] = links.send(rows_in.at[r, 1, 1, :, later], rows_in.at[r, 2, 1, :, later], xm)

    act_x = {}

    def gate_up(r):
        relay_x[r, 0].wait_recv()
        relay_x[r, 1].wait_recv()
        links.settle_all_but(KEEP)
        both = jnp.dot(
            rows_in[r, :, 0].reshape(4 * PAIR, 4 * STRIP), w_gu[0], preferred_element_type=F32
        ) + jnp.dot(
            rows_in[r, :, 1].reshape(4 * PAIR, 4 * STRIP), w_gu[1], preferred_element_type=F32
        )
        left, right = both[:, :384], both[:, 384:]
        made = (left / (1.0 + jnp.exp(-left)) * right).astype(BF).reshape(4, PAIR, 384)
        for slot in range(4):
            act[r, lax.rem(x + slot, 4), :, pl.ds(0, 384)] = made[slot]

    def spread_act(r):
        mine = act.at[r, :, :, pl.ds(0, 384)]
        act_x[r] = [
            links.send(mine, act.at[r, :, :, pl.ds((4 - dx) * 384, 384)], xs[dx])
            for dx in ((2, 1, 3) if r == LAST else (1, 3))
        ]

    def relay_act(r):
        for k, (device, slot) in enumerate(((xp, 3), (xm, 1))):
            act_x[r][k].wait_recv()
            half = pl.ds(2 * k, 2)
            act_x[r].append(
                links.send(
                    act.at[r, half, :, pl.ds(slot * 384, 384)], act.at[r, half, :, pl.ds(768, 384)], device
                )
            )

    home = {}

    def down(r):
        final = r == LAST
        for copy in act_x[r][-3 if final else -2:]:
            copy.wait_recv()
        whole = jnp.dot(
            act[r].reshape(4 * PAIR, 1536), w_dn[...], preferred_element_type=F32
        ).astype(BF).reshape(4, PAIR, 1280)
        for core in range(2):
            done[r, core] = whole[:, :, core * STRIP:(core + 1) * STRIP]
        slot = (4 - r) % 4
        if r == 0:
            home[0] = links.send(done.at[0, 1 - c], back.at[0, c], sib)
            back[0, c] = done[0, c]
        elif not final:
            links.send_both(
                [done.at[r, 0], done.at[r, 1]], back.at[slot, c], chip(r), land("home", slot)
            )
        else:
            for dx in (2, 1, 3, 0):
                t = lax.rem(x + dx, 4)
                links.send_both(
                    [done.at[r, 0, t], done.at[r, 1, t]], back.at[slot, c, t], chip(r), land("end", dx)
                )

    ending = (4 - LAST) % 4

    def wait_codes():
        for copy in side["codes"]:
            copy.wait_recv()

    def wait_home():
        for slot in range(4):
            if slot == 0:
                home[0].wait_recv()
            elif slot != ending:
                links.landed(land("home", slot), back.at[slot], sib)


    comb = p_own

    def combine(dx):
        t = lax.rem(x + dx, 4)
        links.settle_through(front[OWN, 0])
        links.settle_through(front[OWN, 1])
        links.landed(land("end", dx), back.at[ending, :, t], sib)
        mixed = lax.dot_general(
            pick(dx, (0, 1, 2, 3)),
            back[:, :, t].reshape(8 * PAIR, STRIP),
            (((0,), (0,)), ((), ())),
            preferred_element_type=F32,
        ).astype(BF)
        comb[dx] = mixed.reshape(2, 128, STRIP)
        if dx:
            links.send_both(
                [comb.at[dx, 0], comb.at[dx, 1]], fin.at[4 - dx, c], chip(0, dx), land("out", 4 - dx)
            )
        else:
            links.send(comb.at[0, 1 - c], fin.at[0, c], sib, land("out", 0))
            fin[0, c] = comb[0, c]

    square = lax.broadcasted_iota(jnp.int32, (128, 128), 0) == lax.broadcasted_iota(
        jnp.int32, (128, 128), 1
    )
    weight = jnp.sum(jnp.where(square, gates[...], 0.0), axis=1, keepdims=True)
    stay = []

    def output(slot):
        if not stay:
            side["hid"].wait_recv()
            links.settle_through(front["shown"])
        stay.append(slot)
        links.landed(land("out", slot), fin.at[0, 1 - c] if slot == 0 else fin.at[slot], sib)
        b = lax.rem(x + slot, 4)
        cols = pl.ds(pl.multiple_of(b * STRIP, 128), STRIP)
        for half, rows in enumerate((hid.at[c], hid_sib)):
            core = c if half == 0 else 1 - c
            total = rows[:, cols] + weight * fin[slot, core].astype(F32)
            res[core, :, cols] = total.astype(BF)
            col = pl.ds(pl.multiple_of((2 * b + core) * STRIP, 128), STRIP)
            keep = pltpu.make_async_copy(
                res.at[core, :, cols], out.at[:, col], local_sems.at[9]
            )
            keep.start()

    step(TO_SIBLING, start_sibling)
    step(DOWN_X, start_dn)
    step(DOWN_Z, share_dn)
    step(DOWN_WAIT, wait_dn)
    step(OWN_TOKENS, own_tokens)
    step(SIBLING_TOKENS, sibling_tokens)
    step(PLACE, place_tokens)
    step(PLACE_X, share_code)
    step(SUM_SEND, reduce_first, OWN)
    step(SUM_AHEAD, reduce_ahead, OWN)
    step(SUM_BEHIND, reduce_behind, OWN)
    step(SUM_END, finish_own, OWN)
    for j in range(n):
        step(SEND_Q, start_q, j)
        step(SEND_D, start_d, j)
        step(Q_BEHIND, on_q_behind, j)
        step(Q_AHEAD, on_q_ahead, j)
        step(Q_ACROSS, on_rq, j)
        step(D_HERE, on_d, j)
        step(Z_BEHIND, on_z, j, 1, given=(j,))
        step(Z_AHEAD, on_z, j, 0, given=(j,))
        step(Z_ACROSS, on_zo, j)
        step(MUL_SIDES, sides, j)
        step(MUL_ACROSS, across, j)
        step(SUM_SEND, reduce_first, j)
        step(SUM_AHEAD, reduce_ahead, j)
        step(SUM_BEHIND, reduce_behind, j)
        step(SUM_END, finish_piece, j)
    step(SQUARES, start_share)
    step(HIDDEN, start_other)
    step(NORM, normalize)
    for r in range(4):
        step(ROWS_Y, dispatch, r)
        step(ROWS_X, spread_rows, r)
        step(ROWS_AHEAD, relay_ahead, r)
        step(ROWS_BEHIND, relay_behind, r)
        step(SHOWN_WAIT, wait_dispatched, r)
        for t in range(4):
            step(SHOWN_Y, dispatch_shown, r, t)
        step(GATE_UP, gate_up, r)
        step(ACT_X, spread_act, r)
        step(ACT_RELAY, relay_act, r)
        step(DOWN, down, r)
        step(COMBINE, combine, r)
        step(OUT, output, r)
    step(HOME, wait_home)
    step(PLACE_WAIT, wait_codes)
    step(SHOW, show_rows)
    step(SHOW_AHEAD, show_on_ahead)
    step(SHOW_BEHIND, show_on_behind)
    step(SHOW_WAIT, wait_shown)
    for key in PLAN:
        steps.pop(key)()
    steps.pop((ACT_RELAY, LAST))
    assert not steps
    pltpu.make_async_copy(out, out, local_sems.at[9]).wait()
    links.settle_all_but(0)


def scratch():
    wide = 3 * WIDE
    return [
        pltpu.VMEM((2, 512, 2048), BF),
        pltpu.VMEM((PIECES, 2048, WIDE), BF),
        pltpu.VMEM((PIECES, 3, 2048, WIDE), BF),
        pltpu.VMEM((2, 128, 4 * STRIP), BF),
        pltpu.VMEM((2, 128, 4 * STRIP), F32),
        pltpu.VMEM((128, 4 * STRIP), F32),
        pltpu.VMEM((4, 2, 128, STRIP), BF),
        pltpu.VMEM((PIECES, 4, 2, 128, wide), BF),
        pltpu.VMEM((2, 128, STRIP), BF),
        pltpu.VMEM((PIECES, 2, 128, wide), BF),
        pltpu.VMEM((2, 2, 128, STRIP), BF),
        pltpu.VMEM((PIECES, 2, 2, 128, wide), BF),
        pltpu.VMEM((2, 128, 128), F32),
        pltpu.VMEM((2, 128, 128), F32),
        pltpu.VMEM((4, 2, 8, 128), jnp.int32),
        pltpu.VMEM((2, 4 * STRIP, 768), BF),
        pltpu.VMEM((1536, 1280), BF),
        pltpu.VMEM((4, 4, 2, PAIR, 4 * STRIP), BF),
        pltpu.VMEM((3, 2, 128, FRONT), BF),
        pltpu.VMEM((4, 4, 2, PAIR, FRONT), BF),
        pltpu.VMEM((4, 4, PAIR, 1536), BF),
        pltpu.VMEM((4, 2, 4, PAIR, STRIP), BF),
        pltpu.VMEM((4, 2, 4, PAIR, STRIP), BF),
        pltpu.VMEM((4, 2, 128, STRIP), BF),
        pltpu.SemaphoreType.DMA((SENDS,)),
        pltpu.SemaphoreType.DMA((LANDINGS,)),
        pltpu.SemaphoreType.DMA((10,)),
    ]


ANY = pl.BlockSpec(memory_space=pl.ANY)
VM = pl.BlockSpec(memory_space=pltpu.VMEM)


def shards(attn, w_out, resid, norm_gain, route_ids, gate_vals, w_gate, w_up, w_down):
    return pl.pallas_call(
        layer,
        out_shape=jax.ShapeDtypeStruct(resid.shape, BF),
        in_specs=[ANY, ANY, ANY, VM, VM, VM, ANY, ANY, ANY],
        out_specs=ANY,
        scratch_shapes=scratch(),
        compiler_params=pltpu.CompilerParams(
            collective_id=0, has_side_effects=True, vmem_limit_bytes=62 * 2**20
        ),
        name="layer",
    )(
        attn,
        w_out,
        resid,
        norm_gain.reshape(1, -1),
        route_ids.reshape(1, -1),
        gate_vals.reshape(1, -1),
        w_gate,
        w_up,
        w_down,
    )


def solution(mesh):
    placed = (
        P(("dp", "expert"), "tensor"),
        P("tensor", "expert"),
        P(("dp", "expert", "tensor"), None),
        P(),
        P(("dp", "expert", "tensor"), None),
        P(("dp", "expert", "tensor"), None),
        P("expert", None, "tensor"),
        P("expert", None, "tensor"),
        P("expert", "tensor", None),
    )
    return jax.shard_map(
        shards,
        mesh=mesh,
        in_specs=placed,
        out_specs=P(("dp", "expert", "tensor"), None),
        check_vma=False,
    )
```

```python
import functools

import jax
import jax.numpy as jnp
from jax import lax
from jax.experimental import pallas as pl
from jax.experimental.pallas import tpu as pltpu
from jax.sharding import PartitionSpec as P

MESH = pl.DeviceIdType.MESH
BF = jnp.bfloat16
F32 = jnp.float32

QN = 336
DN = 2048 - 4 * QN
QH = 176
PIECES = 5
WIDE = 128
STRIP = 640
FRONT = 2 * STRIP


class Place:
    def __init__(self):
        self.z = lax.axis_index("dp")
        self.e = lax.axis_index("expert")
        self.x = lax.axis_index("tensor")
        self.y = self.e // 2
        self.c = self.e % 2

    def at(self, dx=0, dy=0, dz=0, flip=False):
        core = 1 - self.c if flip else self.c
        return (
            lax.rem(self.z + dz, 4),
            lax.rem(self.y + dy, 4) * 2 + core,
            lax.rem(self.x + dx, 4),
        )


class Links:
    def __init__(self, send_sems, recv_sems):
        self.send_sems, self.recv_sems = send_sems, recv_sems
        self.free, self.made, self.landings, self.open = [], 0, 0, []

    def landing(self):
        self.landings += 1
        return self.landings - 1

    def send(self, src, dst, device, landing=None):
        if not self.free:
            self.free.append(self.made)
            self.made += 1
        i = self.free.pop(0)
        copy = pltpu.make_async_remote_copy(
            src_ref=src,
            dst_ref=dst,
            send_sem=self.send_sems.at[i],
            recv_sem=self.recv_sems.at[self.landing() if landing is None else landing],
            device_id=device,
            device_id_type=MESH,
        )
        copy.start()
        self.open.append((copy, i))
        return copy

    def send_both(self, sources, dst, devices, landing):
        for source, device in zip(sources, devices):
            self.send(source, dst, device, landing)

    def landed(self, landing, dst, device):
        pltpu.make_async_remote_copy(
            src_ref=dst,
            dst_ref=dst,
            send_sem=self.send_sems.at[0],
            recv_sem=self.recv_sems.at[landing],
            device_id=device,
            device_id_type=MESH,
        ).wait_recv()

    def settle(self, count):
        done, self.open = self.open[:count], self.open[count:]
        for copy, i in done:
            copy.wait_send()
            self.free.append(i)

    def settle_through(self, last):
        for k, (copy, _) in enumerate(self.open):
            if copy is last:
                self.settle(k + 1)
                return

    def settle_all_but(self, count):
        self.settle(max(0, len(self.open) - count))


def greet(devices):
    for device in devices:
        pl.semaphore_signal(
            pltpu.get_barrier_semaphore(), inc=1, device_id=device, device_id_type=MESH
        )


SENDS = 92
LANDINGS = 167
KEEP = 48
CAP = 24
PAIR = 2 * CAP
LAST = 3
OWN = PIECES
(
    TO_SIBLING, DOWN_X, DOWN_Z, DOWN_WAIT, OWN_TOKENS, SIBLING_TOKENS, PLACE, PLACE_X, PLACE_WAIT, SUM_SEND,
    SUM_AHEAD, SUM_BEHIND, SUM_END, SEND_Q, SEND_D, Q_BEHIND, Q_AHEAD, Q_ACROSS, D_HERE, Z_BEHIND, Z_AHEAD,
    Z_ACROSS, MUL_SIDES, MUL_ACROSS, SQUARES, HIDDEN, NORM, ROWS_Y, ROWS_X, ROWS_AHEAD, ROWS_BEHIND, SHOW,
    SHOW_AHEAD, SHOW_BEHIND, SHOW_WAIT, SHOWN_Y, SHOWN_WAIT, GATE_UP, ACT_X, ACT_RELAY, DOWN, HOME, COMBINE,
    OUT,
) = range(44)
PLAN = (
    (SEND_Q, 0), (TO_SIBLING,), (OWN_TOKENS,), (SEND_Q, 2), (Q_BEHIND, 0), (Q_AHEAD, 0), (DOWN_X,),
    (SEND_Q, 1), (SEND_D, 2), (Q_BEHIND, 2), (Q_AHEAD, 2), (PLACE,), (Z_AHEAD, 0), (SEND_D, 0),
    (Q_BEHIND, 1), (SEND_D, 1), (SIBLING_TOKENS,), (Q_ACROSS, 2), (Q_AHEAD, 1), (SUM_SEND, OWN),
    (Z_BEHIND, 2), (D_HERE, 2), (Z_AHEAD, 2), (Q_ACROSS, 0), (Z_ACROSS, 2), (Z_BEHIND, 1), (SEND_Q, 4),
    (SUM_AHEAD, OWN), (PLACE_X,), (SUM_BEHIND, OWN), (Z_BEHIND, 0), (D_HERE, 0), (Q_ACROSS, 1),
    (MUL_SIDES, 2), (Z_ACROSS, 0), (D_HERE, 1), (MUL_ACROSS, 2), (SUM_SEND, 2), (Q_BEHIND, 4), (Q_AHEAD, 4),
    (SEND_Q, 3), (MUL_SIDES, 0), (Z_AHEAD, 1), (SEND_D, 4), (MUL_ACROSS, 0), (SUM_END, OWN), (SUM_SEND, 0),
    (Z_ACROSS, 1), (Q_ACROSS, 4), (Z_BEHIND, 4), (Z_AHEAD, 4), (SUM_AHEAD, 2), (Q_BEHIND, 3), (Q_AHEAD, 3),
    (SEND_D, 3), (SUM_BEHIND, 2), (PLACE_WAIT,), (MUL_SIDES, 1), (MUL_ACROSS, 1), (SUM_SEND, 1), (D_HERE, 4),
    (Z_ACROSS, 4), (Q_ACROSS, 3), (MUL_SIDES, 4), (Z_BEHIND, 3), (SUM_BEHIND, 0), (SUM_AHEAD, 0),
    (D_HERE, 3), (Z_AHEAD, 3), (SUM_AHEAD, 1), (SUM_BEHIND, 1), (MUL_ACROSS, 4), (Z_ACROSS, 3),
    (SUM_SEND, 4), (MUL_SIDES, 3), (MUL_ACROSS, 3), (SUM_SEND, 3), (SUM_BEHIND, 4), (DOWN_Z,), (SUM_END, 0),
    (SUM_END, 2), (SUM_AHEAD, 4), (SUM_AHEAD, 3), (SUM_BEHIND, 3), (SUM_END, 1), (SUM_END, 4), (SUM_END, 3),
    (SQUARES,), (NORM,), (ROWS_Y, 2), (SHOW,), (ROWS_Y, 0), (SHOWN_Y, 0, 0), (SHOWN_Y, 1, 0), (ROWS_X, 2),
    (SHOWN_Y, 2, 0), (ROWS_Y, 3), (ROWS_Y, 1), (SHOW_BEHIND,), (SHOW_AHEAD,), (SHOWN_Y, 2, 1),
    (ROWS_BEHIND, 2), (ROWS_X, 1), (SHOWN_Y, 2, 3), (ROWS_AHEAD, 2), (SHOW_WAIT,), (ROWS_X, 0),
    (SHOWN_Y, 2, 2), (ROWS_AHEAD, 1), (SHOWN_Y, 1, 2), (SHOWN_Y, 1, 1), (SHOWN_Y, 0, 1), (SHOWN_Y, 1, 3),
    (SHOWN_Y, 0, 3), (SHOWN_Y, 3, 1), (ROWS_BEHIND, 1), (SHOWN_Y, 3, 0), (SHOWN_WAIT, 2), (GATE_UP, 2),
    (ACT_X, 2), (SHOWN_Y, 0, 2), (SHOWN_Y, 3, 3), (ROWS_X, 3), (ACT_RELAY, 2), (ROWS_BEHIND, 0),
    (ROWS_AHEAD, 0), (SHOWN_Y, 3, 2), (ROWS_BEHIND, 3), (ROWS_AHEAD, 3), (SHOWN_WAIT, 1), (SHOWN_WAIT, 0),
    (DOWN_WAIT,), (GATE_UP, 1), (ACT_X, 1), (DOWN, 2), (GATE_UP, 0), (ACT_X, 0), (SHOWN_WAIT, 3),
    (GATE_UP, 3), (ACT_RELAY, 1), (ACT_X, 3), (DOWN, 1), (HIDDEN,), (ACT_RELAY, 0), (DOWN, 3), (DOWN, 0),
    (HOME,), (COMBINE, 2), (COMBINE, 1), (COMBINE, 0), (COMBINE, 3), (OUT, 2), (OUT, 0), (OUT, 3), (OUT, 1),
)


def layer(
    attn, w_out, resid, gain, ids, gates, w_gate, w_up, w_down, out,
    a_buf, w_own, w, res, hid, hid_sib, p_own, parts, l_own, relays, f_own, finals,
    ssq, ssq_sib, code, w_gu, w_dn, rows_in, near, sown, act, done, back, fin,
    send_sems, recv_sems, local_sems,
):
    me = Place()
    z, x, y, c = me.z, me.x, me.y, me.c
    sib = me.at(flip=True)
    xp, xm, xo = me.at(dx=1), me.at(dx=3), me.at(dx=2)
    yp, ym, zp, zm = me.at(dy=1), me.at(dy=3), me.at(dz=1), me.at(dz=3)
    links = Links(send_sems, recv_sems)

    def chip(dy, dx=0):
        return [(z, lax.rem(y + dy, 4) * 2 + core, lax.rem(x + dx, 4)) for core in range(2)]

    zo_, xs = me.at(dz=2), (None, xp, xo, xm)
    friends = [sib, *chip(1), *chip(2), *chip(3), zp, zm, zo_, *chip(0, 1), *chip(0, 2), *chip(0, 3)]
    greet(friends)

    load_w = [
        pltpu.make_async_copy(w_out.at[:, pl.ds(j * WIDE, WIDE)], w_own.at[j], local_sems.at[j])
        for j in range(PIECES)
    ]
    for load in load_w:
        load.start()
    load_a = pltpu.make_async_copy(attn, a_buf.at[c], local_sems.at[5])
    load_a.start()
    for b in range(4):
        col = pl.multiple_of((2 * b + c) * STRIP, 128)
        load = pltpu.make_async_copy(
            resid.at[:, pl.ds(col, STRIP)], res.at[c, :, pl.ds(b * STRIP, STRIP)], local_sems.at[6]
        )
        load.start()

    loads = []
    for half in range(2):
        for b in range(4):
            source = pl.ds((2 * b + half) * STRIP, STRIP)
            target = pl.ds(b * STRIP, STRIP)
            for k, weight in enumerate((w_gate, w_up)):
                loads.append((weight.at[0, source], w_gu.at[half, target, pl.ds(k * 384, 384)]))
    quarter = pl.ds(pl.multiple_of(x * 1280, 128), 1280)
    loads.append((w_down.at[0, :, quarter], w_dn.at[pl.ds(0, 384)]))
    loads = [
        pltpu.make_async_copy(source, target, local_sems.at[7 if k < 16 else 8])
        for k, (source, target) in enumerate(loads)
    ]

    pl.semaphore_wait(pltpu.get_barrier_semaphore(), len(friends))
    for load in loads:
        load.start()

    def rows_q(half=None):
        start = z * QN
        if half is None:
            return pl.ds(pl.multiple_of(start, 16), QN)
        return pl.ds(pl.multiple_of(start + half * QH, 16), QN - QH if half else QH)

    rows_d = pl.ds(4 * QN, DN)

    def rows_dh(half):
        return pl.ds(4 * QN + half * (DN // 2), DN // 2)

    def own(j, rows):
        return w_own.at[j, rows]

    def send_q(j):
        return (
            links.send(own(j, rows_q()), w.at[j, 1, rows_q()], yp),
            links.send(own(j, rows_q()), w.at[j, 0, rows_q()], ym),
        )

    def send_d(j):
        return (
            links.send(own(j, rows_d), w.at[j, 1, rows_d], yp),
            links.send(own(j, rows_d), w.at[j, 0, rows_d], ym),
        )

    n = PIECES
    q, d, zs, zo, side, first, front, lands = ({} for _ in range(8))
    rows_far = pl.ds(pl.multiple_of(lax.rem(z + 2, 4) * QN, 16), QN)

    def land(*key):
        if key not in lands:
            lands[key] = links.landing()
        return lands[key]

    steps = {}

    def step(kind, run, *args, given=None):
        steps[(kind, *(args if given is None else given))] = functools.partial(run, *args)

    loaded = set()

    def need(j):
        if j not in loaded:
            load_w[j].wait()
            loaded.add(j)

    def start_q(j):
        need(j)
        q[j] = send_q(j)

    def start_d(j):
        need(j)
        d[j] = send_d(j)

    def start_sibling():
        side["attn"] = links.send(attn, a_buf.at[c], sib)
        side["resid"] = links.landing()
        for b in range(4):
            col = pl.multiple_of((2 * b + 1 - c) * STRIP, 128)
            links.send(
                resid.at[:, pl.ds(col, STRIP)], res.at[c, :, pl.ds(b * STRIP, STRIP)], sib, side["resid"]
            )

    dn_rows = pl.multiple_of(z * 96, 16)
    dn_x, dn_z = {}, []

    def start_dn():
        for dx in (1, 3, 2):
            column = pl.multiple_of(lax.rem(x + dx, 4) * 1280, 128)
            dn_x[4 - dx] = links.send(
                w_down.at[0, pl.ds(dn_rows, 96), pl.ds(column, 1280)],
                w_dn.at[pl.ds((4 - dx) * 384 + dn_rows, 96)],
                xs[dx],
            )

    def share_dn():
        for slot in (3, 1, 2):
            dn_x[slot].wait_recv()
            piece = w_dn.at[pl.ds(slot * 384 + dn_rows, 96)]
            dn_z.extend(links.send(piece, piece, device) for device in (zp, zm, zo_))

    def wait_dn():
        for copy in dn_z:
            copy.wait_recv()

    def multiply(blocks, part, core, col):
        def step(m, carry):
            rows = pl.ds(pl.multiple_of(m * 256, 256), 256)
            right = blocks[0][...]
            if len(blocks) > 1:
                right = jnp.concatenate([block[...] for block in blocks], axis=1)
            result = jnp.dot(a_buf[core, rows, :], right, preferred_element_type=F32).astype(BF)
            cols = pl.ds(col, right.shape[1])
            part[2 * m, core, :, cols] = result[:128]
            part[2 * m + 1, core, :, cols] = result[128:]
            return carry

        lax.fori_loop(0, 2, step, 0)

    ahead, behind, over = lax.rem(x + 1, 4), lax.rem(x + 3, 4), lax.rem(x + 2, 4)

    def group(j):
        return (p_own, l_own, f_own) if j == OWN else (parts.at[j], relays.at[j], finals.at[j])

    def reduce_first(j):
        part, relay, final = group(j)
        first[j] = (
            links.send(part.at[over, 0], relay.at[0], xp),
            links.send(part.at[over, 1], relay.at[1], xm),
        )
        links.send(part.at[ahead, 1], final.at[0, 1], xp, land(j, "sum"))
        links.send(part.at[behind, 0], final.at[1, 0], xm, land(j, "sum"))

    def reduce_ahead(j):
        part, relay, final = group(j)
        first[j][0].wait_recv()
        part[ahead, 0] = (part[ahead, 0].astype(F32) + relay[0].astype(F32)).astype(BF)
        front[j, 0] = links.send(part.at[ahead, 0], final.at[0, 0], xp, land(j, "sum"))

    def reduce_behind(j):
        part, relay, final = group(j)
        first[j][1].wait_recv()
        part[behind, 1] = (part[behind, 1].astype(F32) + relay[1].astype(F32)).astype(BF)
        front[j, 1] = links.send(part.at[behind, 1], final.at[1, 1], xm, land(j, "sum"))

    def on_q_behind(j):
        q[j][0].wait_recv()
        links.send(w.at[j, 1, rows_q(0)], w.at[j, 2, rows_q(0)], yp, land(j, "rq"))
        zs[j, 1] = (
            links.send(w.at[j, 1, rows_q()], w.at[j, 1, rows_q()], zp),
            links.send(w.at[j, 1, rows_q()], w.at[j, 1, rows_q()], zm),
        )

    def on_q_ahead(j):
        q[j][1].wait_recv()
        links.send(w.at[j, 0, rows_q(1)], w.at[j, 2, rows_q(1)], ym, land(j, "rq"))
        zs[j, 0] = (
            links.send(w.at[j, 0, rows_q()], w.at[j, 0, rows_q()], zp),
            links.send(w.at[j, 0, rows_q()], w.at[j, 0, rows_q()], zm),
        )

    def on_rq(j):
        links.landed(land(j, "rq"), w.at[j, 2, rows_q()], yp)
        zo[j] = (
            links.send(w.at[j, 2, rows_q()], w.at[j, 2, rows_q()], zp),
            links.send(w.at[j, 2, rows_q()], w.at[j, 2, rows_q()], zm),
        )

    def on_d(j):
        d[j][0].wait_recv()
        links.send(w.at[j, 1, rows_dh(0)], w.at[j, 2, rows_dh(0)], yp, land(j, "rd"))
        d[j][1].wait_recv()
        links.send(w.at[j, 0, rows_dh(1)], w.at[j, 2, rows_dh(1)], ym, land(j, "rd"))

    def z_relay(j, pair, slot):
        low = pl.ds(pl.multiple_of(lax.rem(z + 3, 4) * QN, 16), QH)
        high = pl.ds(pl.multiple_of(lax.rem(z + 1, 4) * QN + QH, 16), QN - QH)
        pair[0].wait_recv()
        links.send(w.at[j, slot, low], w.at[j, slot, low], zp, land(j, slot))
        pair[1].wait_recv()
        links.send(w.at[j, slot, high], w.at[j, slot, high], zm, land(j, slot))

    def on_z(j, slot):
        z_relay(j, zs[j, slot], slot)

    def on_zo(j):
        z_relay(j, zo[j], 2)

    def sides(j):
        links.landed(land(j, 0), w.at[j, 0, rows_far], zp)
        links.landed(land(j, 1), w.at[j, 1, rows_far], zp)
        for core in range(2):
            multiply([w.at[j, 0], w.at[j, 1]], parts.at[j], core, 0)

    def across(j):
        links.landed(land(j, "rd"), w.at[j, 2, rows_d], yp)
        links.landed(land(j, 2), w.at[j, 2, rows_far], zp)
        links.settle_all_but(KEEP)
        for core in range(2):
            multiply([w.at[j, 2]], parts.at[j], core, 2 * WIDE)

    own_pieces = [w_own.at[j] for j in range(PIECES)]

    def own_tokens():
        load_a.wait()
        for j in range(n):
            need(j)
        multiply(own_pieces, p_own, c, 0)

    def sibling_tokens():
        side["attn"].wait_recv()
        multiply(own_pieces, p_own, 1 - c, 0)

    def place_tokens():
        experts = lax.broadcasted_iota(jnp.int32, (8, 128), 0)
        named = ids[...] == experts
        counts = named.astype(F32)
        before = lax.broadcasted_iota(jnp.int32, (128, 128), 0) < lax.broadcasted_iota(
            jnp.int32, (128, 128), 1
        )
        earlier = jnp.dot(counts.astype(BF), before.astype(F32).astype(BF), preferred_element_type=F32)
        slots = jnp.sum(jnp.where(named, earlier, 0.0), axis=0, keepdims=True).astype(jnp.int32)
        code[0, c] = jnp.broadcast_to(ids[...] * PAIR + c * CAP + slots, (8, 128))
        side["code"] = links.send(code.at[0, c], code.at[0, c], sib)

    def share_code():
        side["code"].wait_recv()
        side["codes"] = [links.send(code.at[0], code.at[4 - dx], xs[dx]) for dx in (1, 3, 2)]

    def finish(j, strips, width):
        part, _, final = group(j)
        links.landed(land(j, "sum"), final, xp)
        for k, (col, strip) in enumerate(strips):
            cols = pl.ds(col, width)
            for core in range(2):
                at = pl.ds(k * width, width)
                total = (
                    res[core, :, cols].astype(F32)
                    + part[x, core, :, at].astype(F32)
                    + final[0, core, :, at].astype(F32)
                    + final[1, core, :, at].astype(F32)
                )
                hid[core, :, cols] = total
                add = jnp.sum(total * total, axis=1, keepdims=True)
                ssq[core] = ssq[core] + jnp.broadcast_to(add, (128, 128))

    ssq[...] = jnp.zeros_like(ssq)

    def finish_piece(j):
        strips = [
            (pl.multiple_of(lax.rem(y + dy, 4) * STRIP + j * WIDE, 128), k)
            for k, dy in enumerate((1, 3, 2))
        ]
        finish(j, strips, WIDE)

    def finish_own(_):
        pltpu.make_async_copy(res.at[c], res.at[c], local_sems.at[6]).wait()
        links.landed(side["resid"], res.at[1 - c], sib)
        finish(OWN, [(pl.multiple_of(y * STRIP, 128), 0)], STRIP)

    def start_share():
        side["ssq"] = links.send(ssq, ssq_sib, sib)

    def start_other():
        side["hid"] = links.send(hid.at[1 - c], hid_sib, sib)


    def pick(slot, chips):
        blocks = []
        for dy in chips:
            base = lax.rem(y + dy, 4) * (2 * PAIR)
            place = base + lax.broadcasted_iota(jnp.int32, (2 * PAIR, 128), 0)
            blocks.append(
                jnp.concatenate(
                    [
                        (place == code[slot, core, 0:1, :]).astype(F32).astype(BF)
                        for core in range(2)
                    ],
                    axis=1,
                )
            )
        return blocks[0] if len(blocks) == 1 else jnp.concatenate(blocks, axis=0)

    def normalize():
        side["ssq"].wait_recv()
        for core in range(2):
            scale = lax.rsqrt((ssq[core] + ssq_sib[core])[:, 0:1] / 5120.0 + 1e-06)
            for b in range(4):
                cols = pl.ds(b * STRIP, STRIP)
                col = pl.multiple_of((2 * b + c) * STRIP, 128)
                res[core, :, cols] = (hid[core, :, cols] * scale * gain[0:1, pl.ds(col, STRIP)]).astype(BF)
        pltpu.make_async_copy(w_gu, w_gu, local_sems.at[7]).wait()
        loads[16].wait()
        links.settle_all_but(KEEP)

    arrive, come, shown = {}, {}, []
    early, later = pl.ds(0, FRONT), pl.ds(FRONT, FRONT)

    def sent(dy, core):
        return a_buf.at[0, pl.ds(pl.multiple_of((2 * dy + core) * PAIR, 16), PAIR), early]

    def dispatch(r):
        dy = (4 - r) % 4
        choice = pick(0, (dy,))
        normed = res[:, :, later].reshape(256, FRONT)
        rows = jnp.dot(choice, normed, preferred_element_type=F32).astype(BF)
        a_buf[0, pl.ds(2 * dy * PAIR, 2 * PAIR), early] = rows
        slot = (4 - dy) % 4
        if dy == 0:
            arrive[0] = links.send(sent(0, 1 - c), rows_in.at[0, 0, c, :, later], sib)
            rows_in[0, 0, c, :, later] = sent(0, c)[...]
        else:
            target = rows_in.at[slot, 0, c, :, later]
            links.send_both([sent(dy, 0), sent(dy, 1)], target, chip(dy), land("rows", slot))

    spread, relay_x = {}, {}

    def show_rows():
        shown.append(links.send(res.at[:, :, early], near.at[2], xp))
        shown.append(links.send(res.at[:, :, early], near.at[0], xm))

    def show_on_ahead():
        shown[0].wait_recv()
        come[0] = links.send(near.at[2, 0], near.at[1, 0], xp)

    def show_on_behind():
        shown[1].wait_recv()
        come[1] = links.send(near.at[0, 1], near.at[1, 1], xm)

    def wait_shown():
        come[0].wait_recv()
        come[1].wait_recv()

    def dispatch_shown(r, t):
        dy = (4 - r) % 4
        source = res[:, :, early] if t == 0 else near[t - 1]
        rows = jnp.dot(pick(t, (dy,)), source.reshape(256, FRONT), preferred_element_type=F32)
        sown[r, t] = rows.astype(BF).reshape(2, PAIR, FRONT)
        target = rows_in.at[r, t, c, :, early]
        if r == 0:
            links.send(sown.at[r, t, 1 - c], target, sib, land("shown", r))
            rows_in[r, t, c, :, early] = sown[r, t, c]
        else:
            links.send_both([sown.at[r, t, 0], sown.at[r, t, 1]], target, chip(dy), land("shown", r))

    def wait_dispatched(r):
        links.settle_all_but(KEEP)
        whole = rows_in.at[0, :, 1 - c, :, early] if r == 0 else rows_in.at[r, :, :, :, early]
        links.landed(land("shown", r), whole, sib)

    spread, relay_x = {}, {}

    def spread_rows(r):
        if r == 0:
            arrive[0].wait_recv()
        else:
            links.landed(land("rows", r), rows_in.at[r, 0, :, :, later], sib)
        mine = rows_in.at[r, 0, :, :, later]
        spread[r] = (
            links.send(mine, rows_in.at[r, 3, :, :, later], xp),
            links.send(mine, rows_in.at[r, 1, :, :, later], xm),
        )

    def relay_ahead(r):
        spread[r][0].wait_recv()
        relay_x[r, 0] = links.send(rows_in.at[r, 3, 0, :, later], rows_in.at[r, 2, 0, :, later], xp)

    def relay_behind(r):
        spread[r][1].wait_recv()
        relay_x[r, 1] = links.send(rows_in.at[r, 1, 1, :, later], rows_in.at[r, 2, 1, :, later], xm)

    act_x = {}

    def gate_up(r):
        relay_x[r, 0].wait_recv()
        relay_x[r, 1].wait_recv()
        links.settle_all_but(KEEP)
        both = jnp.dot(
            rows_in[r, :, 0].reshape(4 * PAIR, 4 * STRIP), w_gu[0], preferred_element_type=F32
        ) + jnp.dot(
            rows_in[r, :, 1].reshape(4 * PAIR, 4 * STRIP), w_gu[1], preferred_element_type=F32
        )
        left, right = both[:, :384], both[:, 384:]
        made = (left / (1.0 + jnp.exp(-left)) * right).astype(BF).reshape(4, PAIR, 384)
        for slot in range(4):
            act[r, lax.rem(x + slot, 4), :, pl.ds(0, 384)] = made[slot]

    def spread_act(r):
        mine = act.at[r, :, :, pl.ds(0, 384)]
        act_x[r] = [
            links.send(mine, act.at[r, :, :, pl.ds((4 - dx) * 384, 384)], xs[dx])
            for dx in ((2, 1, 3) if r == LAST else (1, 3))
        ]

    def relay_act(r):
        for k, (device, slot) in enumerate(((xp, 3), (xm, 1))):
            act_x[r][k].wait_recv()
            half = pl.ds(2 * k, 2)
            act_x[r].append(
                links.send(
                    act.at[r, half, :, pl.ds(slot * 384, 384)], act.at[r, half, :, pl.ds(768, 384)], device
                )
            )

    home = {}

    def down(r):
        final = r == LAST
        for copy in act_x[r][-3 if final else -2:]:
            copy.wait_recv()
        whole = jnp.dot(
            act[r].reshape(4 * PAIR, 1536), w_dn[...], preferred_element_type=F32
        ).astype(BF).reshape(4, PAIR, 1280)
        for core in range(2):
            done[r, core] = whole[:, :, core * STRIP:(core + 1) * STRIP]
        slot = (4 - r) % 4
        if r == 0:
            home[0] = links.send(done.at[0, 1 - c], back.at[0, c], sib)
            back[0, c] = done[0, c]
        elif not final:
            links.send_both(
                [done.at[r, 0], done.at[r, 1]], back.at[slot, c], chip(r), land("home", slot)
            )
        else:
            for dx in (2, 1, 3, 0):
                t = lax.rem(x + dx, 4)
                links.send_both(
                    [done.at[r, 0, t], done.at[r, 1, t]], back.at[slot, c, t], chip(r), land("end", dx)
                )

    ending = (4 - LAST) % 4

    def wait_codes():
        for copy in side["codes"]:
            copy.wait_recv()

    def wait_home():
        for slot in range(4):
            if slot == 0:
                home[0].wait_recv()
            elif slot != ending:
                links.landed(land("home", slot), back.at[slot], sib)


    comb = p_own

    def combine(dx):
        t = lax.rem(x + dx, 4)
        links.settle_through(front[OWN, 0])
        links.settle_through(front[OWN, 1])
        links.landed(land("end", dx), back.at[ending, :, t], sib)
        mixed = lax.dot_general(
            pick(dx, (0, 1, 2, 3)),
            back[:, :, t].reshape(8 * PAIR, STRIP),
            (((0,), (0,)), ((), ())),
            preferred_element_type=F32,
        ).astype(BF)
        comb[dx] = mixed.reshape(2, 128, STRIP)
        if dx:
            links.send_both(
                [comb.at[dx, 0], comb.at[dx, 1]], fin.at[4 - dx, c], chip(0, dx), land("out", 4 - dx)
            )
        else:
            links.send(comb.at[0, 1 - c], fin.at[0, c], sib, land("out", 0))
            fin[0, c] = comb[0, c]

    square = lax.broadcasted_iota(jnp.int32, (128, 128), 0) == lax.broadcasted_iota(
        jnp.int32, (128, 128), 1
    )
    weight = jnp.sum(jnp.where(square, gates[...], 0.0), axis=1, keepdims=True)
    stay = []

    def output(slot):
        if not stay:
            side["hid"].wait_recv()
        stay.append(slot)
        links.landed(land("out", slot), fin.at[0, 1 - c] if slot == 0 else fin.at[slot], sib)
        b = lax.rem(x + slot, 4)
        cols = pl.ds(pl.multiple_of(b * STRIP, 128), STRIP)
        for half, rows in enumerate((hid.at[c], hid_sib)):
            core = c if half == 0 else 1 - c
            total = rows[:, cols] + weight * fin[slot, core].astype(F32)
            col = pl.ds(pl.multiple_of((2 * b + core) * STRIP, 128), STRIP)
            out[:, col] = total.astype(BF)

    step(TO_SIBLING, start_sibling)
    step(DOWN_X, start_dn)
    step(DOWN_Z, share_dn)
    step(DOWN_WAIT, wait_dn)
    step(OWN_TOKENS, own_tokens)
    step(SIBLING_TOKENS, sibling_tokens)
    step(PLACE, place_tokens)
    step(PLACE_X, share_code)
    step(SUM_SEND, reduce_first, OWN)
    step(SUM_AHEAD, reduce_ahead, OWN)
    step(SUM_BEHIND, reduce_behind, OWN)
    step(SUM_END, finish_own, OWN)
    for j in range(n):
        step(SEND_Q, start_q, j)
        step(SEND_D, start_d, j)
        step(Q_BEHIND, on_q_behind, j)
        step(Q_AHEAD, on_q_ahead, j)
        step(Q_ACROSS, on_rq, j)
        step(D_HERE, on_d, j)
        step(Z_BEHIND, on_z, j, 1, given=(j,))
        step(Z_AHEAD, on_z, j, 0, given=(j,))
        step(Z_ACROSS, on_zo, j)
        step(MUL_SIDES, sides, j)
        step(MUL_ACROSS, across, j)
        step(SUM_SEND, reduce_first, j)
        step(SUM_AHEAD, reduce_ahead, j)
        step(SUM_BEHIND, reduce_behind, j)
        step(SUM_END, finish_piece, j)
    step(SQUARES, start_share)
    step(HIDDEN, start_other)
    step(NORM, normalize)
    for r in range(4):
        step(ROWS_Y, dispatch, r)
        step(ROWS_X, spread_rows, r)
        step(ROWS_AHEAD, relay_ahead, r)
        step(ROWS_BEHIND, relay_behind, r)
        step(SHOWN_WAIT, wait_dispatched, r)
        for t in range(4):
            step(SHOWN_Y, dispatch_shown, r, t)
        step(GATE_UP, gate_up, r)
        step(ACT_X, spread_act, r)
        step(ACT_RELAY, relay_act, r)
        step(DOWN, down, r)
        step(COMBINE, combine, r)
        step(OUT, output, r)
    step(HOME, wait_home)
    step(PLACE_WAIT, wait_codes)
    step(SHOW, show_rows)
    step(SHOW_AHEAD, show_on_ahead)
    step(SHOW_BEHIND, show_on_behind)
    step(SHOW_WAIT, wait_shown)
    for key in PLAN:
        steps.pop(key)()
    steps.pop((ACT_RELAY, LAST))
    assert not steps
    links.settle_all_but(0)


def scratch():
    wide = 3 * WIDE
    return [
        pltpu.VMEM((2, 512, 2048), BF),
        pltpu.VMEM((PIECES, 2048, WIDE), BF),
        pltpu.VMEM((PIECES, 3, 2048, WIDE), BF),
        pltpu.VMEM((2, 128, 4 * STRIP), BF),
        pltpu.VMEM((2, 128, 4 * STRIP), F32),
        pltpu.VMEM((128, 4 * STRIP), F32),
        pltpu.VMEM((4, 2, 128, STRIP), BF),
        pltpu.VMEM((PIECES, 4, 2, 128, wide), BF),
        pltpu.VMEM((2, 128, STRIP), BF),
        pltpu.VMEM((PIECES, 2, 128, wide), BF),
        pltpu.VMEM((2, 2, 128, STRIP), BF),
        pltpu.VMEM((PIECES, 2, 2, 128, wide), BF),
        pltpu.VMEM((2, 128, 128), F32),
        pltpu.VMEM((2, 128, 128), F32),
        pltpu.VMEM((4, 2, 8, 128), jnp.int32),
        pltpu.VMEM((2, 4 * STRIP, 768), BF),
        pltpu.VMEM((1536, 1280), BF),
        pltpu.VMEM((4, 4, 2, PAIR, 4 * STRIP), BF),
        pltpu.VMEM((3, 2, 128, FRONT), BF),
        pltpu.VMEM((4, 4, 2, PAIR, FRONT), BF),
        pltpu.VMEM((4, 4, PAIR, 1536), BF),
        pltpu.VMEM((4, 2, 4, PAIR, STRIP), BF),
        pltpu.VMEM((4, 2, 4, PAIR, STRIP), BF),
        pltpu.VMEM((4, 2, 128, STRIP), BF),
        pltpu.SemaphoreType.DMA((SENDS,)),
        pltpu.SemaphoreType.DMA((LANDINGS,)),
        pltpu.SemaphoreType.DMA((9,)),
    ]


ANY = pl.BlockSpec(memory_space=pl.ANY)
VM = pl.BlockSpec(memory_space=pltpu.VMEM)


def shards(attn, w_out, resid, norm_gain, route_ids, gate_vals, w_gate, w_up, w_down):
    return pl.pallas_call(
        layer,
        out_shape=pltpu.VMEM(resid.shape, BF),
        in_specs=[ANY, ANY, ANY, VM, VM, VM, ANY, ANY, ANY],
        out_specs=VM,
        scratch_shapes=scratch(),
        compiler_params=pltpu.CompilerParams(
            collective_id=0, has_side_effects=True, vmem_limit_bytes=62 * 2**20
        ),
        name="layer",
    )(
        attn,
        w_out,
        resid,
        norm_gain.reshape(1, -1),
        route_ids.reshape(1, -1),
        gate_vals.reshape(1, -1),
        w_gate,
        w_up,
        w_down,
    )


def solution(mesh):
    placed = (
        P(("dp", "expert"), "tensor"),
        P("tensor", "expert"),
        P(("dp", "expert", "tensor"), None),
        P(),
        P(("dp", "expert", "tensor"), None),
        P(("dp", "expert", "tensor"), None),
        P("expert", None, "tensor"),
        P("expert", None, "tensor"),
        P("expert", "tensor", None),
    )
    return jax.shard_map(
        shards,
        mesh=mesh,
        in_specs=placed,
        out_specs=P(("dp", "expert", "tensor"), None),
        check_vma=False,
    )
```

```python
import functools

import jax
import jax.numpy as jnp
from jax import lax
from jax.experimental import pallas as pl
from jax.experimental.pallas import tpu as pltpu
from jax.sharding import PartitionSpec as P

MESH = pl.DeviceIdType.MESH
BF = jnp.bfloat16
F32 = jnp.float32

QN = 336
DN = 2048 - 4 * QN
QH = 176
PIECES = 5
WIDE = 128
STRIP = 640
FRONT = 2 * STRIP


class Place:
    def __init__(self):
        self.z = lax.axis_index("dp")
        self.e = lax.axis_index("expert")
        self.x = lax.axis_index("tensor")
        self.y = self.e // 2
        self.c = self.e % 2

    def at(self, dx=0, dy=0, dz=0, flip=False):
        core = 1 - self.c if flip else self.c
        return (
            lax.rem(self.z + dz, 4),
            lax.rem(self.y + dy, 4) * 2 + core,
            lax.rem(self.x + dx, 4),
        )


class Links:
    def __init__(self, send_sems, recv_sems):
        self.send_sems, self.recv_sems = send_sems, recv_sems
        self.free, self.made, self.landings, self.open = [], 0, 0, []

    def landing(self):
        self.landings += 1
        return self.landings - 1

    def send(self, src, dst, device, landing=None):
        if not self.free:
            self.free.append(self.made)
            self.made += 1
        i = self.free.pop(0)
        copy = pltpu.make_async_remote_copy(
            src_ref=src,
            dst_ref=dst,
            send_sem=self.send_sems.at[i],
            recv_sem=self.recv_sems.at[self.landing() if landing is None else landing],
            device_id=device,
            device_id_type=MESH,
        )
        copy.start()
        self.open.append((copy, i))
        return copy

    def send_both(self, sources, dst, devices, landing):
        for source, device in zip(sources, devices):
            self.send(source, dst, device, landing)

    def landed(self, landing, dst, device):
        pltpu.make_async_remote_copy(
            src_ref=dst,
            dst_ref=dst,
            send_sem=self.send_sems.at[0],
            recv_sem=self.recv_sems.at[landing],
            device_id=device,
            device_id_type=MESH,
        ).wait_recv()

    def settle(self, count):
        done, self.open = self.open[:count], self.open[count:]
        for copy, i in done:
            copy.wait_send()
            self.free.append(i)

    def settle_through(self, last):
        for k, (copy, _) in enumerate(self.open):
            if copy is last:
                self.settle(k + 1)
                return

    def settle_all_but(self, count):
        self.settle(max(0, len(self.open) - count))


def greet(devices):
    for device in devices:
        pl.semaphore_signal(
            pltpu.get_barrier_semaphore(), inc=1, device_id=device, device_id_type=MESH
        )


SENDS = 80
LANDINGS = 157
KEEP = 36
CAP = 24
PAIR = 2 * CAP
LAST = 3
OWN = PIECES
(
    TO_SIBLING, DOWN_X, DOWN_Z, DOWN_WAIT, OWN_TOKENS, SIBLING_TOKENS, PLACE, PLACE_X, PLACE_WAIT, SUM_SEND,
    SUM_AHEAD, SUM_BEHIND, SUM_END, SEND_Q, SEND_D, Q_BEHIND, Q_AHEAD, Q_ACROSS, D_HERE, Z_BEHIND, Z_AHEAD,
    Z_ACROSS, MUL_SIDES, MUL_ACROSS, SQUARES, HIDDEN, NORM, ROWS_Y, ROWS_X, ROWS_AHEAD, ROWS_BEHIND, SHOW,
    SHOW_AHEAD, SHOW_BEHIND, SHOW_WAIT, SHOWN_Y, SHOWN_WAIT, GATE_UP, ACT_X, ACT_RELAY, DOWN, HOME, COMBINE,
    OUT,
) = range(44)
PLAN = (
    (SEND_Q, 0), (TO_SIBLING,), (OWN_TOKENS,), (SEND_Q, 2), (Q_BEHIND, 0), (Q_AHEAD, 0), (DOWN_X,),
    (SEND_Q, 1), (SEND_D, 2), (Q_BEHIND, 2), (Q_AHEAD, 2), (PLACE,), (Z_AHEAD, 0), (SEND_D, 0),
    (Q_BEHIND, 1), (SEND_D, 1), (SIBLING_TOKENS,), (Q_ACROSS, 2), (Q_AHEAD, 1), (SUM_SEND, OWN),
    (Z_BEHIND, 2), (D_HERE, 2), (Z_AHEAD, 2), (Q_ACROSS, 0), (Z_ACROSS, 2), (Z_BEHIND, 1), (SEND_Q, 4),
    (SUM_AHEAD, OWN), (PLACE_X,), (SUM_BEHIND, OWN), (Z_BEHIND, 0), (D_HERE, 0), (Q_ACROSS, 1),
    (MUL_SIDES, 2), (Z_ACROSS, 0), (D_HERE, 1), (MUL_ACROSS, 2), (SUM_SEND, 2), (Q_BEHIND, 4), (Q_AHEAD, 4),
    (SEND_Q, 3), (MUL_SIDES, 0), (Z_AHEAD, 1), (SEND_D, 4), (MUL_ACROSS, 0), (SUM_END, OWN), (SUM_SEND, 0),
    (Z_ACROSS, 1), (Q_ACROSS, 4), (Z_BEHIND, 4), (Z_AHEAD, 4), (SUM_AHEAD, 2), (Q_BEHIND, 3), (Q_AHEAD, 3),
    (SEND_D, 3), (SUM_BEHIND, 2), (PLACE_WAIT,), (MUL_SIDES, 1), (MUL_ACROSS, 1), (SUM_SEND, 1), (D_HERE, 4),
    (Z_ACROSS, 4), (Q_ACROSS, 3), (MUL_SIDES, 4), (Z_BEHIND, 3), (SUM_BEHIND, 0), (SUM_AHEAD, 0),
    (D_HERE, 3), (Z_AHEAD, 3), (SUM_AHEAD, 1), (SUM_BEHIND, 1), (MUL_ACROSS, 4), (Z_ACROSS, 3),
    (SUM_SEND, 4), (MUL_SIDES, 3), (MUL_ACROSS, 3), (SUM_SEND, 3), (SUM_BEHIND, 4), (DOWN_Z,), (SUM_END, 0),
    (SUM_END, 2), (SUM_AHEAD, 4), (SUM_AHEAD, 3), (SUM_BEHIND, 3), (SUM_END, 1), (SUM_END, 4), (SUM_END, 3),
    (SQUARES,), (NORM,), (ROWS_Y, 2), (SHOW,), (ROWS_Y, 0), (SHOWN_Y, 0, 0), (SHOWN_Y, 1, 0), (ROWS_X, 2),
    (SHOWN_Y, 2, 0), (ROWS_Y, 3), (ROWS_Y, 1), (SHOW_BEHIND,), (SHOW_AHEAD,), (SHOWN_Y, 2, 1),
    (ROWS_BEHIND, 2), (ROWS_X, 1), (SHOWN_Y, 2, 3), (ROWS_AHEAD, 2), (SHOW_WAIT,), (ROWS_X, 0),
    (SHOWN_Y, 2, 2), (ROWS_AHEAD, 1), (SHOWN_Y, 1, 2), (SHOWN_Y, 1, 1), (SHOWN_Y, 0, 1), (SHOWN_Y, 1, 3),
    (SHOWN_Y, 0, 3), (SHOWN_Y, 3, 1), (ROWS_BEHIND, 1), (SHOWN_Y, 3, 0), (SHOWN_WAIT, 2), (GATE_UP, 2),
    (ACT_X, 2), (SHOWN_Y, 0, 2), (SHOWN_Y, 3, 3), (ROWS_X, 3), (ACT_RELAY, 2), (ROWS_BEHIND, 0),
    (ROWS_AHEAD, 0), (SHOWN_Y, 3, 2), (ROWS_BEHIND, 3), (ROWS_AHEAD, 3), (SHOWN_WAIT, 1), (SHOWN_WAIT, 0),
    (DOWN_WAIT,), (GATE_UP, 1), (ACT_X, 1), (DOWN, 2), (GATE_UP, 0), (ACT_X, 0), (SHOWN_WAIT, 3),
    (GATE_UP, 3), (ACT_RELAY, 1), (ACT_X, 3), (DOWN, 1), (HIDDEN,), (ACT_RELAY, 0), (DOWN, 3), (DOWN, 0),
    (HOME,), (COMBINE, 2), (COMBINE, 1), (COMBINE, 0), (COMBINE, 3), (OUT, 2), (OUT, 0), (OUT, 3), (OUT, 1),
)


def layer(
    attn, w_out, resid, gain, ids, gates, w_gate, w_up, w_down, out,
    a_buf, w_own, w, res, hid, hid_sib, p_own, parts, l_own, relays, f_own, finals,
    ssq, ssq_sib, code, w_gu, w_dn, rows_in, near, sown, act, done, back, fin,
    send_sems, recv_sems, local_sems,
):
    me = Place()
    z, x, y, c = me.z, me.x, me.y, me.c
    sib = me.at(flip=True)
    xp, xm, xo = me.at(dx=1), me.at(dx=3), me.at(dx=2)
    yp, ym, zp, zm = me.at(dy=1), me.at(dy=3), me.at(dz=1), me.at(dz=3)
    links = Links(send_sems, recv_sems)

    def chip(dy, dx=0):
        return [(z, lax.rem(y + dy, 4) * 2 + core, lax.rem(x + dx, 4)) for core in range(2)]

    zo_, xs = me.at(dz=2), (None, xp, xo, xm)
    friends = [sib, *chip(1), *chip(2), *chip(3), zp, zm, zo_, *chip(0, 1), *chip(0, 2), *chip(0, 3)]
    greet(friends)

    load_w = [
        pltpu.make_async_copy(w_out.at[:, pl.ds(j * WIDE, WIDE)], w_own.at[j], local_sems.at[j])
        for j in range(PIECES)
    ]
    for load in load_w:
        load.start()
    load_a = pltpu.make_async_copy(attn, a_buf.at[c], local_sems.at[5])
    load_a.start()
    for b in range(4):
        col = pl.multiple_of((2 * b + c) * STRIP, 128)
        load = pltpu.make_async_copy(
            resid.at[:, pl.ds(col, STRIP)], res.at[c, :, pl.ds(b * STRIP, STRIP)], local_sems.at[6]
        )
        load.start()

    loads = []
    for half in range(2):
        for b in range(4):
            source = pl.ds((2 * b + half) * STRIP, STRIP)
            target = pl.ds(b * STRIP, STRIP)
            for k, weight in enumerate((w_gate, w_up)):
                loads.append((weight.at[0, source], w_gu.at[half, target, pl.ds(k * 384, 384)]))
    quarter = pl.ds(pl.multiple_of(x * 1280, 128), 1280)
    loads.append((w_down.at[0, :, quarter], w_dn.at[pl.ds(0, 384)]))
    loads = [
        pltpu.make_async_copy(source, target, local_sems.at[7 if k < 16 else 8])
        for k, (source, target) in enumerate(loads)
    ]

    pl.semaphore_wait(pltpu.get_barrier_semaphore(), len(friends))
    for load in loads:
        load.start()

    def rows_q(half=None):
        start = z * QN
        if half is None:
            return pl.ds(pl.multiple_of(start, 16), QN)
        return pl.ds(pl.multiple_of(start + half * QH, 16), QN - QH if half else QH)

    rows_d = pl.ds(4 * QN, DN)

    def rows_dh(half):
        return pl.ds(4 * QN + half * (DN // 2), DN // 2)

    def own(j, rows):
        return w_own.at[j, rows]

    def send_q(j):
        return (
            links.send(own(j, rows_q()), w.at[j, 1, rows_q()], yp),
            links.send(own(j, rows_q()), w.at[j, 0, rows_q()], ym),
        )

    def send_d(j):
        return (
            links.send(own(j, rows_d), w.at[j, 1, rows_d], yp, land(j, "d")),
            links.send(own(j, rows_d), w.at[j, 0, rows_d], ym, land(j, "d")),
        )

    n = PIECES
    q, d, zs, zo, side, first, front, lands = ({} for _ in range(8))
    rows_far = pl.ds(pl.multiple_of(lax.rem(z + 2, 4) * QN, 16), QN)

    def land(*key):
        if key not in lands:
            lands[key] = links.landing()
        return lands[key]

    steps = {}

    def step(kind, run, *args, given=None):
        steps[(kind, *(args if given is None else given))] = functools.partial(run, *args)

    loaded = set()

    def need(j):
        if j not in loaded:
            load_w[j].wait()
            loaded.add(j)

    def start_q(j):
        need(j)
        q[j] = send_q(j)

    def start_d(j):
        need(j)
        d[j] = send_d(j)

    def start_sibling():
        side["attn"] = links.send(attn, a_buf.at[c], sib)
        side["resid"] = links.landing()
        for b in range(4):
            col = pl.multiple_of((2 * b + 1 - c) * STRIP, 128)
            links.send(
                resid.at[:, pl.ds(col, STRIP)], res.at[c, :, pl.ds(b * STRIP, STRIP)], sib, side["resid"]
            )

    dn_rows = pl.multiple_of(z * 96, 16)
    dn_x, dn_z = {}, []

    def start_dn():
        for dx in (1, 3, 2):
            column = pl.multiple_of(lax.rem(x + dx, 4) * 1280, 128)
            dn_x[4 - dx] = links.send(
                w_down.at[0, pl.ds(dn_rows, 96), pl.ds(column, 1280)],
                w_dn.at[pl.ds((4 - dx) * 384 + dn_rows, 96)],
                xs[dx],
            )

    def share_dn():
        for slot in (3, 1, 2):
            dn_x[slot].wait_recv()
            piece = w_dn.at[pl.ds(slot * 384 + dn_rows, 96)]
            dn_z.extend(links.send(piece, piece, device) for device in (zp, zm, zo_))

    def wait_dn():
        for copy in dn_z:
            copy.wait_recv()

    def multiply(blocks, part, core, col):
        def step(m, carry):
            rows = pl.ds(pl.multiple_of(m * 256, 256), 256)
            right = blocks[0][...]
            if len(blocks) > 1:
                right = jnp.concatenate([block[...] for block in blocks], axis=1)
            result = jnp.dot(a_buf[core, rows, :], right, preferred_element_type=F32).astype(BF)
            cols = pl.ds(col, right.shape[1])
            part[2 * m, core, :, cols] = result[:128]
            part[2 * m + 1, core, :, cols] = result[128:]
            return carry

        lax.fori_loop(0, 2, step, 0)

    ahead, behind, over = lax.rem(x + 1, 4), lax.rem(x + 3, 4), lax.rem(x + 2, 4)

    def group(j):
        return (p_own, l_own, f_own) if j == OWN else (parts.at[j], relays.at[j], finals.at[j])

    def reduce_first(j):
        part, relay, final = group(j)
        first[j] = (
            links.send(part.at[over, 0], relay.at[0], xp),
            links.send(part.at[over, 1], relay.at[1], xm),
        )
        links.send(part.at[ahead, 1], final.at[0, 1], xp, land(j, "sum"))
        links.send(part.at[behind, 0], final.at[1, 0], xm, land(j, "sum"))

    def reduce_ahead(j):
        part, relay, final = group(j)
        first[j][0].wait_recv()
        part[ahead, 0] = (part[ahead, 0].astype(F32) + relay[0].astype(F32)).astype(BF)
        front[j, 0] = links.send(part.at[ahead, 0], final.at[0, 0], xp, land(j, "sum"))

    def reduce_behind(j):
        part, relay, final = group(j)
        first[j][1].wait_recv()
        part[behind, 1] = (part[behind, 1].astype(F32) + relay[1].astype(F32)).astype(BF)
        front[j, 1] = links.send(part.at[behind, 1], final.at[1, 1], xm, land(j, "sum"))

    def on_q_behind(j):
        q[j][0].wait_recv()
        links.send(w.at[j, 1, rows_q(0)], w.at[j, 2, rows_q(0)], yp, land(j, "rq"))
        zs[j, 1] = (
            links.send(w.at[j, 1, rows_q()], w.at[j, 1, rows_q()], zp),
            links.send(w.at[j, 1, rows_q()], w.at[j, 1, rows_q()], zm),
        )

    def on_q_ahead(j):
        q[j][1].wait_recv()
        links.send(w.at[j, 0, rows_q(1)], w.at[j, 2, rows_q(1)], ym, land(j, "rq"))
        zs[j, 0] = (
            links.send(w.at[j, 0, rows_q()], w.at[j, 0, rows_q()], zp),
            links.send(w.at[j, 0, rows_q()], w.at[j, 0, rows_q()], zm),
        )

    def on_rq(j):
        links.landed(land(j, "rq"), w.at[j, 2, rows_q()], yp)
        zo[j] = (
            links.send(w.at[j, 2, rows_q()], w.at[j, 2, rows_q()], zp),
            links.send(w.at[j, 2, rows_q()], w.at[j, 2, rows_q()], zm),
        )

    def on_d(j):
        links.landed(land(j, "d"), w.at[j, pl.ds(0, 2), rows_d], yp)
        links.send(w.at[j, 1, rows_dh(0)], w.at[j, 2, rows_dh(0)], yp, land(j, "rd"))
        links.send(w.at[j, 0, rows_dh(1)], w.at[j, 2, rows_dh(1)], ym, land(j, "rd"))

    def z_relay(j, pair, slot):
        low = pl.ds(pl.multiple_of(lax.rem(z + 3, 4) * QN, 16), QH)
        high = pl.ds(pl.multiple_of(lax.rem(z + 1, 4) * QN + QH, 16), QN - QH)
        pair[0].wait_recv()
        links.send(w.at[j, slot, low], w.at[j, slot, low], zp, land(j, slot))
        pair[1].wait_recv()
        links.send(w.at[j, slot, high], w.at[j, slot, high], zm, land(j, slot))

    def on_z(j, slot):
        z_relay(j, zs[j, slot], slot)

    def on_zo(j):
        z_relay(j, zo[j], 2)

    def sides(j):
        links.landed(land(j, 0), w.at[j, 0, rows_far], zp)
        links.landed(land(j, 1), w.at[j, 1, rows_far], zp)
        for core in range(2):
            multiply([w.at[j, 0], w.at[j, 1]], parts.at[j], core, 0)

    def across(j):
        links.landed(land(j, "rd"), w.at[j, 2, rows_d], yp)
        links.landed(land(j, 2), w.at[j, 2, rows_far], zp)
        links.settle_all_but(KEEP)
        for core in range(2):
            multiply([w.at[j, 2]], parts.at[j], core, 2 * WIDE)

    own_pieces = [w_own.at[j] for j in range(PIECES)]

    def own_tokens():
        load_a.wait()
        for j in range(n):
            need(j)
        multiply(own_pieces, p_own, c, 0)

    def sibling_tokens():
        side["attn"].wait_recv()
        multiply(own_pieces, p_own, 1 - c, 0)

    def place_tokens():
        experts = lax.broadcasted_iota(jnp.int32, (8, 128), 0)
        named = ids[...] == experts
        counts = named.astype(F32)
        before = lax.broadcasted_iota(jnp.int32, (128, 128), 0) < lax.broadcasted_iota(
            jnp.int32, (128, 128), 1
        )
        earlier = jnp.dot(counts.astype(BF), before.astype(F32).astype(BF), preferred_element_type=F32)
        slots = jnp.sum(jnp.where(named, earlier, 0.0), axis=0, keepdims=True).astype(jnp.int32)
        code[0, c] = jnp.broadcast_to(ids[...] * PAIR + c * CAP + slots, (8, 128))
        side["code"] = links.send(code.at[0, c], code.at[0, c], sib)

    def share_code():
        side["code"].wait_recv()
        side["codes"] = [links.send(code.at[0], code.at[4 - dx], xs[dx]) for dx in (1, 3, 2)]

    def finish(j, strips, width):
        part, _, final = group(j)
        links.landed(land(j, "sum"), final, xp)
        for k, (col, strip) in enumerate(strips):
            cols = pl.ds(col, width)
            for core in range(2):
                at = pl.ds(k * width, width)
                total = (
                    res[core, :, cols].astype(F32)
                    + part[x, core, :, at].astype(F32)
                    + final[0, core, :, at].astype(F32)
                    + final[1, core, :, at].astype(F32)
                )
                hid[core, :, cols] = total
                add = jnp.sum(total * total, axis=1, keepdims=True)
                ssq[core] = ssq[core] + jnp.broadcast_to(add, (128, 128))

    ssq[...] = jnp.zeros_like(ssq)

    def finish_piece(j):
        strips = [
            (pl.multiple_of(lax.rem(y + dy, 4) * STRIP + j * WIDE, 128), k)
            for k, dy in enumerate((1, 3, 2))
        ]
        finish(j, strips, WIDE)

    def finish_own(_):
        pltpu.make_async_copy(res.at[c], res.at[c], local_sems.at[6]).wait()
        links.landed(side["resid"], res.at[1 - c], sib)
        finish(OWN, [(pl.multiple_of(y * STRIP, 128), 0)], STRIP)

    def start_share():
        side["ssq"] = links.send(ssq, ssq_sib, sib)

    def start_other():
        side["hid"] = links.send(hid.at[1 - c], hid_sib, sib)


    def pick(slot, chips):
        blocks = []
        for dy in chips:
            base = lax.rem(y + dy, 4) * (2 * PAIR)
            place = base + lax.broadcasted_iota(jnp.int32, (2 * PAIR, 128), 0)
            blocks.append(
                jnp.concatenate(
                    [
                        (place == code[slot, core, 0:1, :]).astype(F32).astype(BF)
                        for core in range(2)
                    ],
                    axis=1,
                )
            )
        return blocks[0] if len(blocks) == 1 else jnp.concatenate(blocks, axis=0)

    def normalize():
        side["ssq"].wait_recv()
        for core in range(2):
            scale = lax.rsqrt((ssq[core] + ssq_sib[core])[:, 0:1] / 5120.0 + 1e-06)
            for b in range(4):
                cols = pl.ds(b * STRIP, STRIP)
                col = pl.multiple_of((2 * b + c) * STRIP, 128)
                res[core, :, cols] = (hid[core, :, cols] * scale * gain[0:1, pl.ds(col, STRIP)]).astype(BF)
        pltpu.make_async_copy(w_gu, w_gu, local_sems.at[7]).wait()
        loads[16].wait()
        links.settle_all_but(KEEP)

    arrive, come, shown = {}, {}, []
    early, later = pl.ds(0, FRONT), pl.ds(FRONT, FRONT)

    def sent(dy, core):
        return a_buf.at[0, pl.ds(pl.multiple_of((2 * dy + core) * PAIR, 16), PAIR), early]

    def dispatch(r):
        dy = (4 - r) % 4
        choice = pick(0, (dy,))
        normed = res[:, :, later].reshape(256, FRONT)
        rows = jnp.dot(choice, normed, preferred_element_type=F32).astype(BF)
        a_buf[0, pl.ds(2 * dy * PAIR, 2 * PAIR), early] = rows
        slot = (4 - dy) % 4
        if dy == 0:
            arrive[0] = links.send(sent(0, 1 - c), rows_in.at[0, 0, c, :, later], sib)
            rows_in[0, 0, c, :, later] = sent(0, c)[...]
        else:
            target = rows_in.at[slot, 0, c, :, later]
            links.send_both([sent(dy, 0), sent(dy, 1)], target, chip(dy), land("rows", slot))

    spread, relay_x = {}, {}

    def show_rows():
        shown.append(links.send(res.at[:, :, early], near.at[2], xp))
        shown.append(links.send(res.at[:, :, early], near.at[0], xm))

    def show_on_ahead():
        shown[0].wait_recv()
        come[0] = links.send(near.at[2, 0], near.at[1, 0], xp, land("near"))

    def show_on_behind():
        shown[1].wait_recv()
        come[1] = links.send(near.at[0, 1], near.at[1, 1], xm, land("near"))

    def wait_shown():
        links.landed(land("near"), near.at[1], sib)

    def dispatch_shown(r, t):
        dy = (4 - r) % 4
        source = res[:, :, early] if t == 0 else near[t - 1]
        rows = jnp.dot(pick(t, (dy,)), source.reshape(256, FRONT), preferred_element_type=F32)
        sown[r, t] = rows.astype(BF).reshape(2, PAIR, FRONT)
        target = rows_in.at[r, t, c, :, early]
        if r == 0:
            links.send(sown.at[r, t, 1 - c], target, sib, land("shown", r))
            rows_in[r, t, c, :, early] = sown[r, t, c]
        else:
            links.send_both([sown.at[r, t, 0], sown.at[r, t, 1]], target, chip(dy), land("shown", r))

    def wait_dispatched(r):
        links.settle_all_but(KEEP)
        whole = rows_in.at[0, :, 1 - c, :, early] if r == 0 else rows_in.at[r, :, :, :, early]
        links.landed(land("shown", r), whole, sib)

    spread, relay_x = {}, {}

    def spread_rows(r):
        if r == 0:
            arrive[0].wait_recv()
        else:
            links.landed(land("rows", r), rows_in.at[r, 0, :, :, later], sib)
        mine = rows_in.at[r, 0, :, :, later]
        spread[r] = (
            links.send(mine, rows_in.at[r, 3, :, :, later], xp),
            links.send(mine, rows_in.at[r, 1, :, :, later], xm),
        )

    def relay_ahead(r):
        spread[r][0].wait_recv()
        relay_x[r, 0] = links.send(rows_in.at[r, 3, 0, :, later], rows_in.at[r, 2, 0, :, later], xp, land("relay", r))

    def relay_behind(r):
        spread[r][1].wait_recv()
        relay_x[r, 1] = links.send(rows_in.at[r, 1, 1, :, later], rows_in.at[r, 2, 1, :, later], xm, land("relay", r))

    act_x = {}

    def gate_up(r):
        links.landed(land("relay", r), rows_in.at[r, 2, :, :, later], sib)
        links.settle_all_but(KEEP)
        both = jnp.dot(
            rows_in[r, :, 0].reshape(4 * PAIR, 4 * STRIP), w_gu[0], preferred_element_type=F32
        ) + jnp.dot(
            rows_in[r, :, 1].reshape(4 * PAIR, 4 * STRIP), w_gu[1], preferred_element_type=F32
        )
        left, right = both[:, :384], both[:, 384:]
        made = (left / (1.0 + jnp.exp(-left)) * right).astype(BF).reshape(4, PAIR, 384)
        for slot in range(4):
            act[r, lax.rem(x + slot, 4), :, pl.ds(0, 384)] = made[slot]

    def spread_act(r):
        mine = act.at[r, :, :, pl.ds(0, 384)]
        act_x[r] = [
            links.send(mine, act.at[r, :, :, pl.ds((4 - dx) * 384, 384)], xs[dx])
            for dx in ((2, 1, 3) if r == LAST else (1, 3))
        ]

    def relay_act(r):
        for k, (device, slot) in enumerate(((xp, 3), (xm, 1))):
            act_x[r][k].wait_recv()
            half = pl.ds(2 * k, 2)
            act_x[r].append(
                links.send(
                    act.at[r, half, :, pl.ds(slot * 384, 384)], act.at[r, half, :, pl.ds(768, 384)], device
                )
            )

    home = {}

    def down(r):
        final = r == LAST
        for copy in act_x[r][-3 if final else -2:]:
            copy.wait_recv()
        whole = jnp.dot(
            act[r].reshape(4 * PAIR, 1536), w_dn[...], preferred_element_type=F32
        ).astype(BF).reshape(4, PAIR, 1280)
        for core in range(2):
            done[r, core] = whole[:, :, core * STRIP:(core + 1) * STRIP]
        slot = (4 - r) % 4
        if r == 0:
            home[0] = links.send(done.at[0, 1 - c], back.at[0, c], sib)
            back[0, c] = done[0, c]
        elif not final:
            links.send_both(
                [done.at[r, 0], done.at[r, 1]], back.at[slot, c], chip(r), land("home", slot)
            )
        else:
            for dx in (2, 1, 3, 0):
                t = lax.rem(x + dx, 4)
                links.send_both(
                    [done.at[r, 0, t], done.at[r, 1, t]], back.at[slot, c, t], chip(r), land("end", dx)
                )

    ending = (4 - LAST) % 4

    def wait_codes():
        for copy in side["codes"]:
            copy.wait_recv()

    def wait_home():
        for slot in range(4):
            if slot == 0:
                home[0].wait_recv()
            elif slot != ending:
                links.landed(land("home", slot), back.at[slot], sib)


    comb = p_own

    def combine(dx):
        t = lax.rem(x + dx, 4)
        links.settle_through(front[OWN, 0])
        links.settle_through(front[OWN, 1])
        links.landed(land("end", dx), back.at[ending, :, t], sib)
        mixed = lax.dot_general(
            pick(dx, (0, 1, 2, 3)),
            back[:, :, t].reshape(8 * PAIR, STRIP),
            (((0,), (0,)), ((), ())),
            preferred_element_type=F32,
        ).astype(BF)
        comb[dx] = mixed.reshape(2, 128, STRIP)
        if dx:
            links.send_both(
                [comb.at[dx, 0], comb.at[dx, 1]], fin.at[4 - dx, c], chip(0, dx), land("out", 4 - dx)
            )
        else:
            links.send(comb.at[0, 1 - c], fin.at[0, c], sib, land("out", 0))
            fin[0, c] = comb[0, c]

    square = lax.broadcasted_iota(jnp.int32, (128, 128), 0) == lax.broadcasted_iota(
        jnp.int32, (128, 128), 1
    )
    weight = jnp.sum(jnp.where(square, gates[...], 0.0), axis=1, keepdims=True)
    stay = []

    def output(slot):
        if not stay:
            side["hid"].wait_recv()
        stay.append(slot)
        links.landed(land("out", slot), fin.at[0, 1 - c] if slot == 0 else fin.at[slot], sib)
        b = lax.rem(x + slot, 4)
        cols = pl.ds(pl.multiple_of(b * STRIP, 128), STRIP)
        for half, rows in enumerate((hid.at[c], hid_sib)):
            core = c if half == 0 else 1 - c
            total = rows[:, cols] + weight * fin[slot, core].astype(F32)
            col = pl.ds(pl.multiple_of((2 * b + core) * STRIP, 128), STRIP)
            out[:, col] = total.astype(BF)

    step(TO_SIBLING, start_sibling)
    step(DOWN_X, start_dn)
    step(DOWN_Z, share_dn)
    step(DOWN_WAIT, wait_dn)
    step(OWN_TOKENS, own_tokens)
    step(SIBLING_TOKENS, sibling_tokens)
    step(PLACE, place_tokens)
    step(PLACE_X, share_code)
    step(SUM_SEND, reduce_first, OWN)
    step(SUM_AHEAD, reduce_ahead, OWN)
    step(SUM_BEHIND, reduce_behind, OWN)
    step(SUM_END, finish_own, OWN)
    for j in range(n):
        step(SEND_Q, start_q, j)
        step(SEND_D, start_d, j)
        step(Q_BEHIND, on_q_behind, j)
        step(Q_AHEAD, on_q_ahead, j)
        step(Q_ACROSS, on_rq, j)
        step(D_HERE, on_d, j)
        step(Z_BEHIND, on_z, j, 1, given=(j,))
        step(Z_AHEAD, on_z, j, 0, given=(j,))
        step(Z_ACROSS, on_zo, j)
        step(MUL_SIDES, sides, j)
        step(MUL_ACROSS, across, j)
        step(SUM_SEND, reduce_first, j)
        step(SUM_AHEAD, reduce_ahead, j)
        step(SUM_BEHIND, reduce_behind, j)
        step(SUM_END, finish_piece, j)
    step(SQUARES, start_share)
    step(HIDDEN, start_other)
    step(NORM, normalize)
    for r in range(4):
        step(ROWS_Y, dispatch, r)
        step(ROWS_X, spread_rows, r)
        step(ROWS_AHEAD, relay_ahead, r)
        step(ROWS_BEHIND, relay_behind, r)
        step(SHOWN_WAIT, wait_dispatched, r)
        for t in range(4):
            step(SHOWN_Y, dispatch_shown, r, t)
        step(GATE_UP, gate_up, r)
        step(ACT_X, spread_act, r)
        step(ACT_RELAY, relay_act, r)
        step(DOWN, down, r)
        step(COMBINE, combine, r)
        step(OUT, output, r)
    step(HOME, wait_home)
    step(PLACE_WAIT, wait_codes)
    step(SHOW, show_rows)
    step(SHOW_AHEAD, show_on_ahead)
    step(SHOW_BEHIND, show_on_behind)
    step(SHOW_WAIT, wait_shown)
    for key in PLAN:
        steps.pop(key)()
    steps.pop((ACT_RELAY, LAST))
    assert not steps
    links.settle_all_but(0)


def scratch():
    wide = 3 * WIDE
    return [
        pltpu.VMEM((2, 512, 2048), BF),
        pltpu.VMEM((PIECES, 2048, WIDE), BF),
        pltpu.VMEM((PIECES, 3, 2048, WIDE), BF),
        pltpu.VMEM((2, 128, 4 * STRIP), BF),
        pltpu.VMEM((2, 128, 4 * STRIP), F32),
        pltpu.VMEM((128, 4 * STRIP), F32),
        pltpu.VMEM((4, 2, 128, STRIP), BF),
        pltpu.VMEM((PIECES, 4, 2, 128, wide), BF),
        pltpu.VMEM((2, 128, STRIP), BF),
        pltpu.VMEM((PIECES, 2, 128, wide), BF),
        pltpu.VMEM((2, 2, 128, STRIP), BF),
        pltpu.VMEM((PIECES, 2, 2, 128, wide), BF),
        pltpu.VMEM((2, 128, 128), F32),
        pltpu.VMEM((2, 128, 128), F32),
        pltpu.VMEM((4, 2, 8, 128), jnp.int32),
        pltpu.VMEM((2, 4 * STRIP, 768), BF),
        pltpu.VMEM((1536, 1280), BF),
        pltpu.VMEM((4, 4, 2, PAIR, 4 * STRIP), BF),
        pltpu.VMEM((3, 2, 128, FRONT), BF),
        pltpu.VMEM((4, 4, 2, PAIR, FRONT), BF),
        pltpu.VMEM((4, 4, PAIR, 1536), BF),
        pltpu.VMEM((4, 2, 4, PAIR, STRIP), BF),
        pltpu.VMEM((4, 2, 4, PAIR, STRIP), BF),
        pltpu.VMEM((4, 2, 128, STRIP), BF),
        pltpu.SemaphoreType.DMA((SENDS,)),
        pltpu.SemaphoreType.DMA((LANDINGS,)),
        pltpu.SemaphoreType.DMA((9,)),
    ]


ANY = pl.BlockSpec(memory_space=pl.ANY)
VM = pl.BlockSpec(memory_space=pltpu.VMEM)


def shards(attn, w_out, resid, norm_gain, route_ids, gate_vals, w_gate, w_up, w_down):
    return pl.pallas_call(
        layer,
        out_shape=pltpu.VMEM(resid.shape, BF),
        in_specs=[ANY, ANY, ANY, VM, VM, VM, ANY, ANY, ANY],
        out_specs=VM,
        scratch_shapes=scratch(),
        compiler_params=pltpu.CompilerParams(
            collective_id=0, has_side_effects=True, vmem_limit_bytes=62 * 2**20
        ),
        name="layer",
    )(
        attn,
        w_out,
        resid,
        norm_gain.reshape(1, -1),
        route_ids.reshape(1, -1),
        gate_vals.reshape(1, -1),
        w_gate,
        w_up,
        w_down,
    )


def solution(mesh):
    placed = (
        P(("dp", "expert"), "tensor"),
        P("tensor", "expert"),
        P(("dp", "expert", "tensor"), None),
        P(),
        P(("dp", "expert", "tensor"), None),
        P(("dp", "expert", "tensor"), None),
        P("expert", None, "tensor"),
        P("expert", None, "tensor"),
        P("expert", "tensor", None),
    )
    return jax.shard_map(
        shards,
        mesh=mesh,
        in_specs=placed,
        out_specs=P(("dp", "expert", "tensor"), None),
        check_vma=False,
    )
```
